128 devices in a mesh: lon: 16 (over x, z_lo, core), mem: 8 (over z_hi, y).
Axes of the slice: x: 4, y: 4, z: 4 (z_hi: 2, z_lo: 2; z = z_hi * 2 + z_lo), core: 2. Of those that a mesh axis runs over, the one named last changes fastest.
Arguments:
- inputs: bfloat16 [8, 2, 96, 192, 192], P('mem', None, None, 'lon'), may hold values from -6 to 6
- target: bfloat16 [2, 96, 192, 192], P(None, None, 'lon'), may hold values from -8 to 8
- norm_gain_vector: float32 [192], replicated, may hold values from 0.1 to 1.9
- w_qkv: bfloat16 [192, 576], replicated, may hold values from -0.4375 to 0.4375
- w_proj: bfloat16 [192, 192], replicated, may hold values from -0.4375 to 0.4375
- lat_region: int32 [96], replicated, may hold values from 0 to 31, never falling along the last dimension, each value on 1 to 6 neighbouring positions
- lat_valid: int32 [96], replicated, may hold values 0 or 1
Outputs:
- grad_inputs: bfloat16 [8, 2, 96, 192, 192], P('mem', None, None, 'lon')
- grad_qkv: float32 [192, 576], replicated
- grad_proj: float32 [192, 192], replicated
- grad_gain: float32 [192], replicated
- loss: float32 [], replicated
The draws below stay inside these ranges and needn't reach their ends.
Inputs may be any that keep to these rules, and one draw needn't show every extreme that they name: `lat_region`: never falls along the rows; each value covers 1 to 6 consecutive rows, and every value of the range occurs.
All inputs are finite; a program needn't handle non-finite values.
Results may differ from the reference program's by a relative error of at most 0.015.
Values may be sent and summed in bfloat16 or wider, within the bound.
No kernel may reach another device: no remote copies, remote signals or barrier semaphores. Data moves between devices by JAX's collectives and lax.ppermute only.
A program may use at most 128 MiB of HBM per device.

```python
import math
import jax
import jax.numpy as jnp
import numpy as np
from jax import lax

C = 192
HEADS = 6
LEV = 2
SHIFT = 6
LATP = 96
M = 8
NLON = 192
NTOK = 294912


def place_ends(entries, stream_key, smallest, largest):
    longest = entries.shape.index(max(entries.shape))
    spots = []
    for shift in (0, 1):
        where = [jax.random.randint(jax.random.fold_in(stream_key, axis), (), 0, length) for axis, length in enumerate(entries.shape)]
        where[longest] = (where[longest] + shift) % entries.shape[longest]
        spots.append(tuple(where))
    return entries.at[spots[0]].set(smallest).at[spots[1]].set(largest)


def steps_of(stream_key, shape, cuts, smallest, top_value):
    def one(position, shards_of):
        heights = jax.random.uniform(jax.random.fold_in(jax.random.fold_in(stream_key, 6), position), (shards_of,), jnp.float32, smallest / len(cuts), top_value / len(cuts))
        return jnp.repeat(jnp.exp(heights), shape[position] // shards_of).reshape((-1,) + (1,) * (len(shape) - position - 1))

    factor_of = one(*cuts[0])
    for cut in cuts[1:]:
        factor_of = factor_of * one(*cut)
    return factor_of


def length_profile(number_of, total, most, skew):
    weights = [(1 << 20) // math.isqrt(standing ** skew) + 1 for standing in range(2, number_of + 1)]
    rest, counts = total - most - (number_of - 1), [1] * (number_of - 1)
    while rest > 0:
        movable = [i for i in range(number_of - 1) if counts[i] < most]
        whole, remaining = sum([weights[i] for i in movable]), rest
        for i in movable:
            more = min(most - counts[i], max(1, remaining * weights[i] // whole), rest)
            counts[i] = counts[i] + more
            rest = rest - more
    return np.array([most] + counts)


def ragged(key, amount, total, bound, slope):
    if amount == 2:
        one = jax.random.randint(key, (), max(1, total - bound), min(bound, total - 1) + 1)
        return jnp.stack([one, total - one])
    sizes = jnp.asarray(length_profile(amount, total, bound, slope), jnp.int32)
    couples = (amount - 1) // 2
    giver, sink = sizes[1:1 + 2 * couples:2], sizes[2:2 + 2 * couples:2]
    slack = jnp.minimum(giver - 1, bound - sink)
    moved = jax.random.randint(jax.random.fold_in(key, 1), (couples,), 0, 1 << 20) % (slack + 1)
    sizes = sizes.at[1:1 + 2 * couples:2].set(giver - moved).at[2:2 + 2 * couples:2].set(sink + moved)
    return sizes[jax.random.permutation(jax.random.fold_in(key, 2), amount)]


def centred(stream_key, shape, scale, bound, shards=(), kind=jnp.bfloat16):
    entries = scale * jax.random.normal(stream_key, shape, jnp.float32)
    if shards:
        entries = entries * steps_of(stream_key, shape, shards, -0.22, 0.18)
    return jnp.clip(entries, -bound, bound).astype(kind)


def setup_inputs(seed: int = 0) -> dict:
    seeds = jax.random.split(jax.random.key(seed), 8)
    return {
        "inputs": centred(seeds[0], (M, LEV, LATP, NLON, C), 1.0, 6.0, ((0, 8), (3, 16))),
        "target": centred(seeds[1], (LEV, LATP, NLON, C), 1.5, 8.0, ((2, 16),)),
        "norm_gain_vector": jnp.clip(1.0 + 0.18 * jax.random.normal(seeds[2], (C,), jnp.float32), 0.1, 1.9),
        "w_qkv": centred(seeds[3], (C, 3 * C), C ** -0.5, 0.4375),
        "w_proj": centred(seeds[4], (C, C), C ** -0.5, 0.4375),
        "lat_region": jnp.searchsorted(jnp.cumsum(ragged(seeds[5], LATP // 3, LATP, 6, 0)), jnp.arange(LATP), side="right").astype(jnp.int32),
        "lat_valid": place_ends((jax.random.randint(seeds[6], (LATP,), 0, 8) < 7).astype(jnp.int32), jax.random.fold_in(seeds[6], 1), 0, 1),
    }


EPS = 1e-05
DELTA_SQ = 0.0625

def to_windows(field):
    levels, rows, columns, width = field.shape
    field = field.reshape(levels // 2, 2, rows // 6, 6, columns // 12, 12, width)
    field = field.transpose(0, 2, 4, 1, 3, 5, 6)
    return field.reshape(levels // 2, rows // 6, columns // 12, 144, width)

def from_windows(field, levels, rows, columns):
    width = field.shape[-1]
    field = field.reshape(levels // 2, rows // 6, columns // 12, 2, 6, 12, width)
    field = field.transpose(0, 3, 1, 4, 2, 5, 6)
    return field.reshape(levels, rows, columns, width)

def window_mask(lat_region, lat_valid):
    blocks = lat_region.shape[0] // 6
    region = jnp.broadcast_to(lat_region.reshape(blocks, 1, 6, 1), (blocks, 2, 6, 12)).reshape(blocks, 144)
    valid = jnp.broadcast_to(lat_valid.reshape(blocks, 1, 6, 1), (blocks, 2, 6, 12)).reshape(blocks, 144)
    same = region[:, :, None] == region[:, None, :]
    itself = jnp.arange(144)[:, None] == jnp.arange(144)[None, :]
    return same & ((valid[:, None, :] == 1) | itself[None])

def batched(spec, left, right):
    return jnp.einsum(spec, left.astype(jnp.float32), right.astype(jnp.float32))

def split_heads(field):
    first, second, cells, width = field.shape
    return field.reshape(first, second, cells, HEADS, width // HEADS).transpose(0, 1, 3, 2, 4)

def merge_heads(field):
    first, second, heads, cells, size = field.shape
    return field.transpose(0, 1, 3, 2, 4).reshape(first, second, cells, heads * size)

def weights_of(query, keys, mask):
    scale = query.shape[-1] ** (-0.5)
    scores = batched('abhqd,abhkd->abhqk', query, keys) * scale
    scores = jnp.where(mask[:, None, None], scores, -1e+30)
    expo = jnp.exp(scores)
    return expo / lax.optimization_barrier(jnp.sum(expo, axis=-1, keepdims=True))

def forward_block(block, w_qkv, mask):
    width = block.shape[-1]
    qkv = jnp.dot(block, w_qkv, preferred_element_type=jnp.float32).astype(jnp.bfloat16)
    query = split_heads(qkv[..., :width])
    keys = split_heads(qkv[..., width:2 * width])
    value_rows = split_heads(qkv[..., 2 * width:])
    probs = weights_of(query, keys, mask).astype(jnp.bfloat16)
    attended = batched('abhqk,abhkd->abhqd', probs, value_rows).astype(jnp.bfloat16)
    return (qkv, merge_heads(attended))

def backward_block(block, qkv, attended, grad_rows, w_qkv, w_proj, mask):
    width = block.shape[-1]
    query = split_heads(qkv[..., :width])
    keys = split_heads(qkv[..., width:2 * width])
    value_rows = split_heads(qkv[..., 2 * width:])
    scale = query.shape[-1] ** (-0.5)
    weights = weights_of(query, keys, mask)
    probs = weights.astype(jnp.bfloat16)
    grad_att = split_heads(jnp.dot(grad_rows, w_proj.T, preferred_element_type=jnp.float32).astype(jnp.bfloat16))
    grad_probs = batched('abhqd,abhkd->abhqk', grad_att, value_rows)
    total = lax.optimization_barrier(jnp.sum(weights * grad_probs, axis=-1, keepdims=True))
    grad_scores = (weights * (grad_probs - total) * scale).astype(jnp.bfloat16)
    grad_query = batched('abhqk,abhkd->abhqd', grad_scores, keys)
    grad_keys = batched('abhqk,abhqd->abhkd', grad_scores, query)
    grad_values = batched('abhqk,abhqd->abhkd', probs, grad_att)
    grad_qkv = jnp.concatenate([merge_heads(grad_query), merge_heads(grad_keys), merge_heads(grad_values)], axis=-1).astype(jnp.bfloat16)
    qkv_part = jnp.dot(block.reshape(-1, width).T, grad_qkv.reshape(-1, 3 * width), preferred_element_type=jnp.float32)
    proj_part = jnp.dot(attended.reshape(-1, width).T, grad_rows.reshape(-1, width), preferred_element_type=jnp.float32)
    grad_block = jnp.dot(grad_qkv, w_qkv.T, preferred_element_type=jnp.float32).astype(jnp.bfloat16)
    return (grad_block, qkv_part, proj_part)

def layer_normalize(inputs, gain_vector):
    value_rows = inputs.astype(jnp.float32)
    mean_removed = value_rows - lax.optimization_barrier(jnp.mean(value_rows, axis=-1, keepdims=True))
    inverse_deviation = lax.rsqrt(lax.optimization_barrier(jnp.mean(mean_removed * mean_removed, axis=-1, keepdims=True)) + EPS)
    standardized_input = mean_removed * inverse_deviation
    return (value_rows, standardized_input, inverse_deviation, (standardized_input * gain_vector).astype(jnp.bfloat16))

def attend_grid(rolled, w_qkv, w_proj, mask):
    levels, rows, columns, width = rolled.shape
    windows = to_windows(rolled)
    qkv, attended = lax.map(lambda block: forward_block(block, w_qkv, mask), windows)
    proj = jnp.dot(attended, w_proj, preferred_element_type=jnp.float32).astype(jnp.bfloat16)
    return (windows, qkv, attended, from_windows(proj, levels, rows, columns))

def backward_grid(windows, qkv, attended, grad_rolled, w_qkv, w_proj, mask):
    levels, rows, columns, width = grad_rolled.shape
    grad_windows = to_windows(grad_rolled)
    grad_blocks, qkv_parts, proj_parts = lax.map(lambda items: backward_block(items[0], items[1], items[2], items[3], w_qkv, w_proj, mask), (windows, qkv, attended, grad_windows))
    return (from_windows(grad_blocks, levels, rows, columns), lax.optimization_barrier(jnp.sum(qkv_parts, axis=0)), lax.optimization_barrier(jnp.sum(proj_parts, axis=0)))

def smooth(diff):
    return jnp.sqrt(diff * diff + DELTA_SQ)

def member_forward(inputs, gain_vector, w_qkv, w_proj, mask):
    value_rows, standardized_input, inverse_deviation, normalized_rows = layer_normalize(inputs, gain_vector)
    rolled = jnp.roll(normalized_rows, -SHIFT, axis=2)
    windows, qkv, attended, proj = attend_grid(rolled, w_qkv, w_proj, mask)
    return value_rows + jnp.roll(proj, SHIFT, axis=2).astype(jnp.float32)

def member_backward(inputs, grad_mixed, gain_vector, w_qkv, w_proj, mask):
    value_rows, standardized_input, inverse_deviation, normalized_rows = layer_normalize(inputs, gain_vector)
    rolled = jnp.roll(normalized_rows, -SHIFT, axis=2)
    windows, qkv, attended, proj = attend_grid(rolled, w_qkv, w_proj, mask)
    grad_rolled = jnp.roll(grad_mixed.astype(jnp.bfloat16), -SHIFT, axis=2)
    grad_back, qkv_part, proj_part = backward_grid(windows, qkv, attended, grad_rolled, w_qkv, w_proj, mask)
    gradient_normalized = jnp.roll(grad_back, SHIFT, axis=2).astype(jnp.float32)
    gain_partial = lax.optimization_barrier(jnp.sum(gradient_normalized * standardized_input, axis=(0, 1, 2)))
    scaled_rows = gradient_normalized * gain_vector
    gradient_input = inverse_deviation * (scaled_rows - lax.optimization_barrier(jnp.mean(scaled_rows, axis=-1, keepdims=True)) - standardized_input * lax.optimization_barrier(jnp.mean(scaled_rows * standardized_input, axis=-1, keepdims=True)))
    return ((grad_mixed + gradient_input).astype(jnp.bfloat16), qkv_part, proj_part, gain_partial)

def reference(inputs, target, norm_gain_vector, w_qkv, w_proj, lat_region, lat_valid):
    mask = window_mask(lat_region, lat_valid)
    mixed = lax.map(lambda member: member_forward(member, norm_gain_vector, w_qkv, w_proj, mask), inputs)
    rounded = lax.optimization_barrier(mixed.astype(jnp.bfloat16))
    members = mixed.shape[0]

    def pair_member(own_rounded):
        own = own_rounded.astype(jnp.float32)

        def step(carry, other):
            diff = own - other.astype(jnp.float32)
            size = smooth(diff)
            return ((carry[0] + size, carry[1] + diff / size), None)
        zeros = jnp.zeros_like(own)
        result, unused = lax.scan(step, (zeros, zeros), rounded)
        return result
    pairs, slopes = lax.map(pair_member, rounded)
    valid = lat_valid.astype(jnp.float32).reshape(1, 1, -1, 1, 1)
    diff = mixed - target.astype(jnp.float32)[None]
    size = smooth(diff)
    grad_mixed = valid * (diff / size - slopes / members)
    score = jnp.sum(valid * (size - pairs / (2.0 * members)))
    grad_inputs, qkv_parts, proj_parts, gain_parts = lax.map(lambda items: member_backward(items[0], items[1], norm_gain_vector, w_qkv, w_proj, mask), (inputs, grad_mixed))
    scale = NTOK ** (-0.5)
    loss = score / (NTOK * C)
    return (grad_inputs, lax.optimization_barrier(jnp.sum(qkv_parts, axis=0)) * scale, lax.optimization_barrier(jnp.sum(proj_parts, axis=0)) * scale, lax.optimization_barrier(jnp.sum(gain_parts, axis=0)) * scale, loss)
```

```python
import functools

import jax
import jax.numpy as jnp
import numpy as np
from jax import lax
from jax.experimental import pallas as pl
from jax.experimental.pallas import tpu as pltpu
from jax.sharding import PartitionSpec as P

HEADS = 6
SIZE = 32
SHIFT = 6
C = 192
CELLS = 144
HALF = 72
M = 8
EPS = 1e-05
DELTA_SQ = 0.0625
PIECE = 216
GRAD_ROWS = 160
ROWS = 2 * PIECE + GRAD_ROWS
BF = jnp.bfloat16
F32 = jnp.float32
VMEM_LIMIT = 56 * 1024 * 1024


def dot(left, right):
    return jnp.dot(left, right, preferred_element_type=F32)


def dot_t(left, right):
    return lax.dot_general(left, right, (((1,), (1,)), ((), ())), preferred_element_type=F32)


def identity(n):
    return (
        lax.broadcasted_iota(jnp.int32, (n, n), 0) == lax.broadcasted_iota(jnp.int32, (n, n), 1)
    ).astype(BF)


def pack_half(first, second):
    pad = jnp.zeros((HALF, 64), F32)
    rest = jnp.concatenate([first[:, 128:], pad], axis=1)
    other = jnp.concatenate([second[:, 128:], pad], axis=1)
    return jnp.concatenate(
        [first[:, :128], second[:, :128], rest + pltpu.roll(other, 64, 1)], axis=0
    )


def unpack_half(piece, block):
    rest = piece[2 * HALF :]
    if block == 1:
        rest = pltpu.roll(rest, 64, 1)
    return jnp.concatenate([piece[block * HALF : (block + 1) * HALF], rest[:, :64]], axis=1)


def place_matrix():
    cell = np.arange(CELLS)
    half, level, row, column = cell // 72, cell // 36 % 2, cell // 6 % 6, cell % 6
    out = np.zeros((CELLS, 12 * 16), np.float32)
    out[cell, (level * 6 + row) * 16 + half * 6 + column] = 1.0
    return out


def pack_kernel(x_ref, t_ref, place_ref, x_out, t_out, slabs):
    @pl.when(pl.program_id(0) == 0)
    def _():
        slabs[...] = jnp.zeros_like(slabs)

    def gather(ref):
        blocks = []
        for block in range(2):
            for level in range(2):
                for row in range(6):
                    at = (level * 6 + row) * 16
                    slabs[block, at : at + 12, :] = ref[level, block * 6 + row]
            blocks.append(dot(place_ref[...], slabs[block]))
        return [
            pack_half(blocks[0][half * HALF : (half + 1) * HALF], blocks[1][half * HALF : (half + 1) * HALF]).astype(BF)
            for half in range(2)
        ]

    to_west, own = gather(x_ref.at[0])
    x_out[0, 0] = to_west
    x_out[0, 1] = own

    @pl.when(pl.program_id(0) == 0)
    def _():
        to_west, own = gather(t_ref)
        t_out[0] = to_west
        t_out[1] = own


def pack(inputs, target_rows, place):
    return pl.pallas_call(
        pack_kernel,
        grid=(M,),
        in_specs=[
            pl.BlockSpec((1, 2, 12, 12, C), lambda i: (0, 0, i, 0, 0)),
            pl.BlockSpec((2, 12, 12, C), lambda i: (0, 0, 0, 0)),
            pl.BlockSpec((CELLS, 192), lambda i: (0, 0)),
        ],
        out_specs=[
            pl.BlockSpec((1, 2, PIECE, 128), lambda i: (i, 0, 0, 0)),
            pl.BlockSpec((2, PIECE, 128), lambda i: (0, 0, 0)),
        ],
        out_shape=[
            jax.ShapeDtypeStruct((M, 2, PIECE, 128), BF),
            jax.ShapeDtypeStruct((2, PIECE, 128), BF),
        ],
        scratch_shapes=[pltpu.VMEM((2, 192, C), BF)],
        name="pack_strip",
    )(inputs, target_rows, place)


def unpack_kernel(own_ref, beyond_ref, place_ref, out_ref):
    own = own_ref[0].astype(F32)
    beyond = beyond_ref[0].astype(F32)
    for block in range(2):
        cells = jnp.concatenate([unpack_half(beyond, block), unpack_half(own, block)], axis=0).astype(BF)
        slabs = dot(place_ref[...], cells).astype(BF)
        for level in range(2):
            for row in range(6):
                at = (level * 6 + row) * 16
                out_ref[0, level, block * 6 + row] = slabs[at : at + 12, :]


def unpack(own, beyond, place_t):
    return pl.pallas_call(
        unpack_kernel,
        grid=(M,),
        in_specs=[
            pl.BlockSpec((1, PIECE, 128), lambda i: (i, 0, 0)),
            pl.BlockSpec((1, PIECE, 128), lambda i: (i, 0, 0)),
            pl.BlockSpec((192, CELLS), lambda i: (0, 0)),
        ],
        out_specs=pl.BlockSpec((1, 2, 12, 12, C), lambda i: (0, 0, i, 0, 0)),
        out_shape=jax.ShapeDtypeStruct((1, 2, 96, 12, C), BF),
        name="unpack_strip",
    )(own, beyond, place_t)


def head_only(field, head):
    lane = lax.broadcasted_iota(jnp.int32, field.shape, 1)
    return jnp.where((lane >= head * SIZE) & (lane < (head + 1) * SIZE), field, jnp.zeros_like(field))


def main_kernel(
    xo_ref, xb_ref, t_ref, bias_ref, valid_ref, gain_ref, wkv_ref, wqkv_ref, wqkvt_ref, wproj_ref, wprojt_ref,
    out_ref,
    x_s, t_s, xhat_s, rstd_s, n_s, v_s, qkvt_s, att_s, w_s, mixed_s, sqkv_s, sproj_s, sgain_s,
):
    scale = SIZE ** (-0.5)
    to_exp2 = scale * 1.4426950408889634
    gain = gain_ref[...]
    eye_cells = identity(CELLS)
    eye_c = identity(C)

    for member in range(M):
        own = xo_ref[member].astype(F32)
        beyond = xb_ref[member].astype(F32)
        for block in range(2):
            x_s[block * M + member] = jnp.concatenate(
                [unpack_half(own, block), unpack_half(beyond, block)], axis=0
            )
    own = t_ref[0].astype(F32)
    beyond = t_ref[1].astype(F32)
    for block in range(2):
        t_s[block] = jnp.concatenate([unpack_half(own, block), unpack_half(beyond, block)], axis=0)

    def forward(window, carry):
        block = window // M
        x = x_s[window]
        centred = x - jnp.mean(x, axis=1, keepdims=True)
        rstd = lax.rsqrt(jnp.mean(centred * centred, axis=1, keepdims=True) + EPS)
        xhat = centred * rstd
        xhat_s[window] = xhat
        rstd_s[window] = rstd
        normed = (xhat * gain).astype(BF)
        n_s[window] = normed
        kv = dot(normed, wkv_ref[...]).astype(BF)
        keys = kv[:, :C]
        v_s[window] = kv[:, C:]
        qkvt = dot_t(wqkvt_ref[...], normed).astype(BF)
        qkvt_s[window] = qkvt
        qt = qkvt[:C]
        bias = bias_ref[block]
        parts = []
        for head in range(HEADS):
            scores = dot(head_only(keys, head), qt)
            expo = jnp.exp2(scores * to_exp2 + bias)
            weights = expo * (1.0 / jnp.sum(expo, axis=0, keepdims=True))
            w_s[window, head] = weights
            vt = qkvt[2 * C + head * SIZE : 2 * C + (head + 1) * SIZE]
            parts.append(dot(vt, weights.astype(BF)))
        attended = jnp.concatenate(parts, axis=0).astype(BF)
        att_s[window] = attended
        projt = dot(wprojt_ref[...], attended).astype(BF)
        mixed_s[window] = x + dot_t(eye_cells, projt)
        return carry

    lax.fori_loop(0, 2 * M, forward, 0)

    def crps(step, score):
        block = step // 18
        rows = pl.ds(pl.multiple_of((step % 18) * 8, 8), 8)
        valid = valid_ref[block, rows]
        target = t_s[block, rows]
        mixed = [mixed_s[block * M + m, rows] for m in range(M)]
        rounded = [value.astype(BF).astype(F32) for value in mixed]
        slopes = [None] * M
        pairs = None
        for m in range(M):
            for n in range(m + 1, M):
                diff = rounded[m] - rounded[n]
                square = diff * diff + DELTA_SQ
                inverse = lax.rsqrt(square)
                size = square * inverse
                slope = diff * inverse
                pairs = size if pairs is None else pairs + size
                slopes[m] = slope if slopes[m] is None else slopes[m] + slope
                slopes[n] = -slope if slopes[n] is None else slopes[n] - slope
        total = -(2.0 * pairs + M * DELTA_SQ**0.5) / (2.0 * M)
        for m in range(M):
            diff = mixed[m] - target
            square = diff * diff + DELTA_SQ
            inverse = lax.rsqrt(square)
            total = total + square * inverse
            mixed_s[block * M + m, rows] = valid * (diff * inverse - slopes[m] / M)
        return score + valid * total

    score = lax.fori_loop(0, 36, crps, jnp.zeros((8, C), F32))

    sqkv_s[...] = jnp.zeros_like(sqkv_s)
    sproj_s[...] = jnp.zeros_like(sproj_s)
    sgain_s[...] = jnp.zeros_like(sgain_s)

    def backward(window, carry):
        grad_mixed = mixed_s[window]
        grad_rows = grad_mixed.astype(BF)
        attended = att_s[window]
        gat = dot_t(wproj_ref[...], grad_rows).astype(BF)
        sproj_s[...] += dot(attended, grad_rows)
        values = v_s[window]
        dq, dk, dv = [], [], []
        for head in range(HEADS):
            at = slice(head * SIZE, (head + 1) * SIZE)
            weights = w_s[window, head]
            grad_probs = dot(head_only(values, head), gat)
            total = jnp.sum(weights * grad_probs, axis=0, keepdims=True)
            grad_scores = (weights * ((grad_probs - total) * scale)).astype(BF)
            qt = qkvt_s[window, head * SIZE : (head + 1) * SIZE]
            kt = qkvt_s[window, C + head * SIZE : C + (head + 1) * SIZE]
            dq.append(dot(kt, grad_scores))
            dk.append(dot_t(qt, grad_scores))
            dv.append(dot_t(gat[at], weights.astype(BF)))
        grad_qkvt = jnp.concatenate(dq + dk + dv, axis=0).astype(BF)
        sqkv_s[...] += dot(grad_qkvt, n_s[window])
        gbt = dot(wqkv_ref[...], grad_qkvt).astype(BF)
        grad_normed = dot_t(eye_cells, gbt)
        xhat = xhat_s[window]
        sgain_s[...] += jnp.sum((grad_normed * xhat).reshape(18, 8, C), axis=0)
        scaled = grad_normed * gain
        first = jnp.mean(scaled, axis=1, keepdims=True)
        second = jnp.mean(scaled * xhat, axis=1, keepdims=True)
        x_s[window] = grad_mixed + rstd_s[window] * (scaled - first - xhat * second)
        return carry

    lax.fori_loop(0, 2 * M, backward, 0)

    sqkv = dot_t(eye_c, sqkv_s[...].astype(BF))
    sproj = sproj_s[...]
    pad = jnp.zeros((C, 64), F32)
    rest = jnp.concatenate([sqkv[:, 512:], pad], axis=1)
    rest = rest[:96] + pltpu.roll(rest[96:], 64, 1)
    last = jnp.concatenate([sproj[:, 128:], pad], axis=1)
    last = last[:96] + pltpu.roll(last[96:], 64, 1)
    sgain = jnp.sum(sgain_s[...], axis=0, keepdims=True)
    total = jnp.sum(jnp.sum(score, axis=0, keepdims=True), axis=1, keepdims=True)
    high = total.astype(BF).astype(F32)
    low = (total - high).astype(BF).astype(F32)
    row = lax.broadcasted_iota(jnp.int32, (128, 128), 0)
    lane = lax.broadcasted_iota(jnp.int32, (128, 128), 1)
    extra = jnp.where(row == 0, jnp.broadcast_to(sgain[:, :128], (128, 128)), 0.0)
    wide = jnp.concatenate([sgain[:, 128:], jnp.zeros((1, 64), F32)], axis=1)
    extra = extra + jnp.where(row == 1, jnp.broadcast_to(wide, (128, 128)), 0.0)
    extra = extra + jnp.where((row == 2) & (lane == 0), jnp.broadcast_to(high, (128, 128)), 0.0)
    extra = extra + jnp.where((row == 2) & (lane == 1), jnp.broadcast_to(low, (128, 128)), 0.0)
    grads = jnp.concatenate(
        [sqkv[:, 128 * i : 128 * (i + 1)] for i in range(4)] + [rest, sproj[:, :128], last, extra], axis=0
    )
    for member in range(M):
        halves = []
        for half in range(2):
            at = slice(half * HALF, (half + 1) * HALF)
            halves.append(pack_half(x_s[member, at], x_s[M + member, at]))
        mine = grads[member * GRAD_ROWS : (member + 1) * GRAD_ROWS]
        out_ref[member] = jnp.concatenate(halves + [mine], axis=0).astype(BF)


def main(own, beyond, target, bias, valid, gain, w_qkv, w_proj):
    windows = 2 * M
    return pl.pallas_call(
        main_kernel,
        out_shape=jax.ShapeDtypeStruct((M, ROWS, 128), BF),
        scratch_shapes=[
            pltpu.VMEM((windows, CELLS, C), F32),
            pltpu.VMEM((2, CELLS, C), F32),
            pltpu.VMEM((windows, CELLS, C), F32),
            pltpu.VMEM((windows, CELLS, 1), F32),
            pltpu.VMEM((windows, CELLS, C), BF),
            pltpu.VMEM((windows, CELLS, C), BF),
            pltpu.VMEM((windows, 3 * C, CELLS), BF),
            pltpu.VMEM((windows, C, CELLS), BF),
            pltpu.VMEM((windows, HEADS, CELLS, CELLS), F32),
            pltpu.VMEM((windows, CELLS, C), F32),
            pltpu.VMEM((3 * C, C), F32),
            pltpu.VMEM((C, C), F32),
            pltpu.VMEM((8, C), F32),
        ],
        compiler_params=pltpu.CompilerParams(vmem_limit_bytes=VMEM_LIMIT),
        name="window_attention_crps",
    )(own, beyond, target, bias, valid, gain[None], w_qkv[:, C:], w_qkv, w_qkv.T, w_proj, w_proj.T)


def cell_rows(rows):
    return jnp.broadcast_to(rows.reshape(2, 1, 6, 1), (2, 4, 6, 6)).reshape(2, CELLS)


def body(inputs, target, norm_gain_vector, w_qkv, w_proj, lat_region, lat_valid):
    strips = lax.axis_size("lon")
    mine = lax.axis_index("mem")
    place = place_matrix()
    start = mine * 12
    target_rows = lax.dynamic_slice_in_dim(target, start, 12, axis=1)
    packed, target_packed = pack(inputs, target_rows, jnp.asarray(place, BF))

    region = cell_rows(lax.dynamic_slice_in_dim(lat_region, start, 12))
    valid = cell_rows(lax.dynamic_slice_in_dim(lat_valid, start, 12))
    same = region[:, :, None] == region[:, None, :]
    itself = np.eye(CELLS, dtype=bool)
    bias = jnp.where(same & ((valid[:, :, None] == 1) | itself[None]), 0.0, -1e30).astype(F32)
    valid_column = valid.astype(F32)[:, :, None]

    west = [(i, (i - 1) % strips) for i in range(strips)]
    east = [(i, (i + 1) % strips) for i in range(strips)]
    target_beyond = lax.ppermute(target_packed[0], "lon", west)
    arrived = lax.all_to_all(packed, "mem", 0, 0, tiled=False)
    beyond = lax.ppermute(arrived[:, 0], "lon", west)
    sent = main(
        arrived[:, 1], beyond, jnp.stack([target_packed[1], target_beyond]), bias, valid_column, norm_gain_vector, w_qkv, w_proj
    )
    back = lax.all_to_all(sent, "mem", 0, 0, tiled=False)
    west_half = lax.ppermute(back[:, PIECE : 2 * PIECE], "lon", east)
    part = jnp.sum(back[:, 2 * PIECE :].astype(F32), axis=0)
    bit = 1
    while bit < strips:
        part = part + lax.ppermute(part, "lon", [(i, i ^ bit) for i in range(strips)])
        bit *= 2
    high = part.astype(BF)
    low = (part - high.astype(F32))[32:48].astype(BF)
    full = jnp.concatenate([high, low], axis=0)
    shared = lax.all_to_all(
        jnp.broadcast_to(full[None], (M, GRAD_ROWS + 16, 128)), "mem", 0, 0, tiled=False
    ).astype(F32)
    grads = shared[:, :GRAD_ROWS].reshape(M * GRAD_ROWS, 128)
    extra = shared[M - 1, 32:48] + shared[M - 1, GRAD_ROWS:]
    grad_inputs = unpack(back[:, :PIECE], west_half, jnp.asarray(place.T, BF))

    count = M * 2 * 96 * 12 * strips
    scale = count ** (-0.5)
    rest = grads[768:864]
    qkv_sum = jnp.concatenate(
        [grads[i * C : (i + 1) * C] for i in range(4)]
        + [jnp.concatenate([rest[:, :64], rest[:, 64:]], axis=0)], axis=1
    )
    last = grads[1056:1152]
    proj_sum = jnp.concatenate(
        [grads[864:1056], jnp.concatenate([last[:, :64], last[:, 64:]], axis=0)], axis=1
    )
    gain_sum = extra[:2].reshape(256)[:C]
    loss = (extra[2, 0] + extra[2, 1]) / (count * C)
    return (grad_inputs, qkv_sum * scale, proj_sum * scale, gain_sum * scale, loss)


def solution(mesh):
    in_specs = (
        P("mem", None, None, "lon", None),
        P(None, None, "lon", None),
        P(),
        P(),
        P(),
        P(),
        P(),
    )
    out_specs = (P("mem", None, None, "lon", None), P(), P(), P(), P())
    return jax.shard_map(body, mesh=mesh, in_specs=in_specs, out_specs=out_specs, check_vma=False)
```

```python
import functools

import jax
import jax.numpy as jnp
import numpy as np
from jax import lax
from jax.experimental import pallas as pl
from jax.experimental.pallas import tpu as pltpu
from jax.sharding import PartitionSpec as P

HEADS = 6
SIZE = 32
SHIFT = 6
C = 192
CELLS = 144
HALF = 72
M = 8
EPS = 1e-05
DELTA_SQ = 0.0625
PIECE = 216
GRAD_ROWS = 160
ROWS = 2 * PIECE + GRAD_ROWS
BF = jnp.bfloat16
F32 = jnp.float32
VMEM_LIMIT = 56 * 1024 * 1024


def dot(left, right):
    return jnp.dot(left, right, preferred_element_type=F32)


def dot_t(left, right):
    return lax.dot_general(left, right, (((1,), (1,)), ((), ())), preferred_element_type=F32)


def identity(n):
    return (
        lax.broadcasted_iota(jnp.int32, (n, n), 0) == lax.broadcasted_iota(jnp.int32, (n, n), 1)
    ).astype(BF)


def pack_half(first, second):
    pad = jnp.zeros((HALF, 64), F32)
    rest = jnp.concatenate([first[:, 128:], pad], axis=1)
    other = jnp.concatenate([second[:, 128:], pad], axis=1)
    return jnp.concatenate(
        [first[:, :128], second[:, :128], rest + pltpu.roll(other, 64, 1)], axis=0
    )


def unpack_half(piece, block):
    rest = piece[2 * HALF :]
    if block == 1:
        rest = pltpu.roll(rest, 64, 1)
    return jnp.concatenate([piece[block * HALF : (block + 1) * HALF], rest[:, :64]], axis=1)


def place_matrix():
    cell = np.arange(CELLS)
    half, level, row, column = cell // 72, cell // 36 % 2, cell // 6 % 6, cell % 6
    out = np.zeros((CELLS, 12 * 16), np.float32)
    out[cell, (level * 6 + row) * 16 + half * 6 + column] = 1.0
    return out


def pack_kernel(x_ref, t_ref, place_ref, x_out, t_out, slabs):
    @pl.when(pl.program_id(0) == 0)
    def _():
        slabs[...] = jnp.zeros_like(slabs)

    def gather(ref):
        blocks = []
        for block in range(2):
            for level in range(2):
                for row in range(6):
                    at = (level * 6 + row) * 16
                    slabs[block, at : at + 12, :] = ref[level, block * 6 + row]
            blocks.append(dot(place_ref[...], slabs[block]))
        return [
            pack_half(blocks[0][half * HALF : (half + 1) * HALF], blocks[1][half * HALF : (half + 1) * HALF]).astype(BF)
            for half in range(2)
        ]

    to_west, own = gather(x_ref.at[0])
    x_out[0, 0] = to_west
    x_out[0, 1] = own

    @pl.when(pl.program_id(0) == 0)
    def _():
        to_west, own = gather(t_ref)
        t_out[0] = to_west
        t_out[1] = own


def pack(inputs, target_rows, place):
    return pl.pallas_call(
        pack_kernel,
        grid=(M,),
        in_specs=[
            pl.BlockSpec((1, 2, 12, 12, C), lambda i: (0, 0, i, 0, 0)),
            pl.BlockSpec((2, 12, 12, C), lambda i: (0, 0, 0, 0)),
            pl.BlockSpec((CELLS, 192), lambda i: (0, 0)),
        ],
        out_specs=[
            pl.BlockSpec((1, 2, PIECE, 128), lambda i: (i, 0, 0, 0)),
            pl.BlockSpec((2, PIECE, 128), lambda i: (0, 0, 0)),
        ],
        out_shape=[
            jax.ShapeDtypeStruct((M, 2, PIECE, 128), BF),
            jax.ShapeDtypeStruct((2, PIECE, 128), BF),
        ],
        scratch_shapes=[pltpu.VMEM((2, 192, C), BF)],
        name="pack_strip",
    )(inputs, target_rows, place)


def unpack_kernel(own_ref, beyond_ref, place_ref, out_ref):
    own = own_ref[0].astype(F32)
    beyond = beyond_ref[0].astype(F32)
    for block in range(2):
        cells = jnp.concatenate([unpack_half(beyond, block), unpack_half(own, block)], axis=0).astype(BF)
        slabs = dot(place_ref[...], cells).astype(BF)
        for level in range(2):
            for row in range(6):
                at = (level * 6 + row) * 16
                out_ref[0, level, block * 6 + row] = slabs[at : at + 12, :]


def unpack(own, beyond, place_t):
    return pl.pallas_call(
        unpack_kernel,
        grid=(M,),
        in_specs=[
            pl.BlockSpec((1, PIECE, 128), lambda i: (i, 0, 0)),
            pl.BlockSpec((1, PIECE, 128), lambda i: (i, 0, 0)),
            pl.BlockSpec((192, CELLS), lambda i: (0, 0)),
        ],
        out_specs=pl.BlockSpec((1, 2, 12, 12, C), lambda i: (0, 0, i, 0, 0)),
        out_shape=jax.ShapeDtypeStruct((1, 2, 96, 12, C), BF),
        name="unpack_strip",
    )(own, beyond, place_t)


def head_only(field, head):
    lane = lax.broadcasted_iota(jnp.int32, field.shape, 1)
    return jnp.where((lane >= head * SIZE) & (lane < (head + 1) * SIZE), field, jnp.zeros_like(field))


def main_kernel(
    xo_ref, xb_ref, t_ref, bias_ref, valid_ref, gain_ref, wkv_ref, wqkv_ref, wqkvt_ref, wproj_ref, wprojt_ref,
    out_ref,
    x_s, t_s, xhat_s, rstd_s, n_s, k_s, v_s, qkvt_s, attf_s, att_s, p_s, mixed_s, gat_s, tot_s, ds_s, grad_s,
    sqkv_s, sproj_s, sgain_s,
):
    scale = SIZE ** (-0.5)
    to_exp2 = scale * 1.4426950408889634
    last = 2 * M - 1

    for member in range(M):
        own = xo_ref[member].astype(F32)
        beyond = xb_ref[member].astype(F32)
        for block in range(2):
            x_s[block * M + member] = jnp.concatenate(
                [unpack_half(own, block), unpack_half(beyond, block)], axis=0
            )
    own = t_ref[0].astype(F32)
    beyond = t_ref[1].astype(F32)
    for block in range(2):
        t_s[block] = jnp.concatenate([unpack_half(own, block), unpack_half(beyond, block)], axis=0)


    def project_qkv(window):
        x = x_s[window]
        centred = x - jnp.mean(x, axis=1, keepdims=True)
        rstd = lax.rsqrt(jnp.mean(centred * centred, axis=1, keepdims=True) + EPS)
        xhat = centred * rstd
        xhat_s[window] = xhat
        rstd_s[window] = rstd
        normed = (xhat * gain_ref[...]).astype(BF)
        n_s[window] = normed
        kv = dot(normed, wkv_ref[...]).astype(BF)
        k_s[window] = kv[:, :C]
        v_s[window] = kv[:, C:]
        qkvt_s[window] = dot_t(wqkvt_ref[...], normed).astype(BF)

    def score_head(window, head):
        scores = dot(head_only(k_s[window], head), qkvt_s[window, :C])
        expo = jnp.exp2(scores * to_exp2 + bias_ref[window // M])
        p_s[window, head] = (expo * (1.0 / jnp.sum(expo, axis=0, keepdims=True))).astype(BF)

    def attend_head(window, head):
        at = slice(head * SIZE, (head + 1) * SIZE)
        attended = dot(qkvt_s[window, 2 * C + head * SIZE : 2 * C + (head + 1) * SIZE], p_s[window, head])
        attf_s[window, at] = attended
        att_s[window, at] = attended.astype(BF)

    def heads(*stages):
        for stage, window in stages:
            for head in range(HEADS):
                stage(window, head)

    def forward(step, carry):
        projt = dot(wprojt_ref[...], att_s[step]).astype(BF)
        heads((attend_head, jnp.minimum(step + 1, last)), (score_head, jnp.minimum(step + 2, last)))
        project_qkv(jnp.minimum(step + 3, last))
        mixed_s[step] = x_s[step] + dot_t(identity(CELLS), projt)
        return carry

    project_qkv(0)
    heads((score_head, 0))
    project_qkv(1)
    heads((attend_head, 0), (score_head, 1))
    project_qkv(2)
    lax.fori_loop(0, 2 * M, forward, 0)

    def crps(step, score):
        block = step // 18
        rows = pl.ds(pl.multiple_of((step % 18) * 8, 8), 8)
        valid = valid_ref[block, rows]
        target = t_s[block, rows]
        mixed = [mixed_s[block * M + m, rows] for m in range(M)]
        rounded = [value.astype(BF).astype(F32) for value in mixed]
        slopes = [None] * M
        pairs = None
        for m in range(M):
            for n in range(m + 1, M):
                diff = rounded[m] - rounded[n]
                square = diff * diff + DELTA_SQ
                inverse = lax.rsqrt(square)
                size = square * inverse
                slope = diff * inverse
                pairs = size if pairs is None else pairs + size
                slopes[m] = slope if slopes[m] is None else slopes[m] + slope
                slopes[n] = -slope if slopes[n] is None else slopes[n] - slope
        total = -(2.0 * pairs + M * DELTA_SQ**0.5) / (2.0 * M)
        for m in range(M):
            diff = mixed[m] - target
            square = diff * diff + DELTA_SQ
            inverse = lax.rsqrt(square)
            total = total + square * inverse
            mixed_s[block * M + m, rows] = valid * (diff * inverse - slopes[m] / M)
        return score + valid * total

    score = lax.fori_loop(0, 36, crps, jnp.zeros((8, C), F32))

    sqkv_s[...] = jnp.zeros_like(sqkv_s)
    sproj_s[...] = jnp.zeros_like(sproj_s)
    sgain_s[...] = jnp.zeros_like(sgain_s)

    def grad_attended(window):
        gat = dot_t(wproj_ref[...], mixed_s[window].astype(BF)).astype(BF)
        gat_s[window] = gat
        product = gat.astype(F32) * attf_s[window]
        for head in range(HEADS):
            tot_s[window, head] = jnp.sum(product[head * SIZE : (head + 1) * SIZE], axis=0, keepdims=True)

    def grad_score_head(window, head):
        grad_probs = dot(head_only(v_s[window], head), gat_s[window])
        ds_s[window % 4, head] = (grad_probs - tot_s[window, head]).astype(BF) * p_s[window, head]

    def grad_qkv_head(window, head):
        at = slice(head * SIZE, (head + 1) * SIZE)
        grad_scores = ds_s[window % 4, head]
        qt = qkvt_s[window, at]
        kt = qkvt_s[window, C + head * SIZE : C + (head + 1) * SIZE]
        grad_s[window, at] = (dot(kt, grad_scores) * scale).astype(BF)
        grad_s[window, C + head * SIZE : C + (head + 1) * SIZE] = (dot_t(qt, grad_scores) * scale).astype(BF)
        grad_s[window, 2 * C + head * SIZE : 2 * C + (head + 1) * SIZE] = dot_t(
            gat_s[window, at], p_s[window, head]
        ).astype(BF)

    def grad_norm(window, gbt):
        grad_normed = dot_t(identity(CELLS), gbt)
        xhat = xhat_s[window]
        sgain_s[...] += jnp.sum((grad_normed * xhat).reshape(18, 8, C), axis=0)
        scaled = grad_normed * gain_ref[...]
        first = jnp.mean(scaled, axis=1, keepdims=True)
        second = jnp.mean(scaled * xhat, axis=1, keepdims=True)
        x_s[window] = mixed_s[window] + rstd_s[window] * (scaled - first - xhat * second)

    def backward(step, carry):
        gbt = dot(wqkv_ref[...], grad_s[step]).astype(BF)
        sqkv_s[...] += dot(grad_s[step], n_s[step])
        sproj_s[...] += dot(att_s[step], mixed_s[step].astype(BF))
        heads((grad_qkv_head, jnp.minimum(step + 1, last)), (grad_score_head, jnp.minimum(step + 2, last)))
        grad_attended(jnp.minimum(step + 3, last))
        grad_norm(step, gbt)
        return carry

    grad_attended(0)
    heads((grad_score_head, 0))
    grad_attended(1)
    heads((grad_qkv_head, 0), (grad_score_head, 1))
    grad_attended(2)
    lax.fori_loop(0, 2 * M, backward, 0)

    sqkv = dot_t(identity(C), sqkv_s[...].astype(BF))
    sproj = sproj_s[...]
    pad = jnp.zeros((C, 64), F32)
    rest = jnp.concatenate([sqkv[:, 512:], pad], axis=1)
    rest = rest[:96] + pltpu.roll(rest[96:], 64, 1)
    proj_rest = jnp.concatenate([sproj[:, 128:], pad], axis=1)
    proj_rest = proj_rest[:96] + pltpu.roll(proj_rest[96:], 64, 1)
    sgain = jnp.sum(sgain_s[...], axis=0, keepdims=True)
    total = jnp.sum(jnp.sum(score, axis=0, keepdims=True), axis=1, keepdims=True)
    high = total.astype(BF).astype(F32)
    low = (total - high).astype(BF).astype(F32)
    row = lax.broadcasted_iota(jnp.int32, (128, 128), 0)
    lane = lax.broadcasted_iota(jnp.int32, (128, 128), 1)
    extra = jnp.where(row == 0, jnp.broadcast_to(sgain[:, :128], (128, 128)), 0.0)
    wide = jnp.concatenate([sgain[:, 128:], jnp.zeros((1, 64), F32)], axis=1)
    extra = extra + jnp.where(row == 1, jnp.broadcast_to(wide, (128, 128)), 0.0)
    extra = extra + jnp.where((row == 2) & (lane == 0), jnp.broadcast_to(high, (128, 128)), 0.0)
    extra = extra + jnp.where((row == 2) & (lane == 1), jnp.broadcast_to(low, (128, 128)), 0.0)
    grads = jnp.concatenate(
        [sqkv[:, 128 * i : 128 * (i + 1)] for i in range(4)] + [rest, sproj[:, :128], proj_rest, extra], axis=0
    )
    for member in range(M):
        halves = []
        for half in range(2):
            at = slice(half * HALF, (half + 1) * HALF)
            halves.append(pack_half(x_s[member, at], x_s[M + member, at]))
        mine = grads[member * GRAD_ROWS : (member + 1) * GRAD_ROWS]
        out_ref[member] = jnp.concatenate(halves + [mine], axis=0).astype(BF)


def main(own, beyond, target, bias, valid, gain, w_qkv, w_proj):
    windows = 2 * M
    return pl.pallas_call(
        main_kernel,
        out_shape=jax.ShapeDtypeStruct((M, ROWS, 128), BF),
        scratch_shapes=[
            pltpu.VMEM((windows, CELLS, C), F32),
            pltpu.VMEM((2, CELLS, C), F32),
            pltpu.VMEM((windows, CELLS, C), F32),
            pltpu.VMEM((windows, CELLS, 1), F32),
            pltpu.VMEM((windows, CELLS, C), BF),
            pltpu.VMEM((windows, CELLS, C), BF),
            pltpu.VMEM((windows, CELLS, C), BF),
            pltpu.VMEM((windows, 3 * C, CELLS), BF),
            pltpu.VMEM((windows, C, CELLS), F32),
            pltpu.VMEM((windows, C, CELLS), BF),
            pltpu.VMEM((windows, HEADS, CELLS, CELLS), BF),
            pltpu.VMEM((windows, CELLS, C), F32),
            pltpu.VMEM((windows, C, CELLS), BF),
            pltpu.VMEM((windows, HEADS, 1, CELLS), F32),
            pltpu.VMEM((4, HEADS, CELLS, CELLS), BF),
            pltpu.VMEM((windows, 3 * C, CELLS), BF),
            pltpu.VMEM((3 * C, C), F32),
            pltpu.VMEM((C, C), F32),
            pltpu.VMEM((8, C), F32),
        ],
        compiler_params=pltpu.CompilerParams(vmem_limit_bytes=VMEM_LIMIT),
        name="window_attention_crps",
    )(own, beyond, target, bias, valid, gain[None], w_qkv[:, C:], w_qkv, w_qkv.T, w_proj, w_proj.T)


def cell_rows(rows):
    return jnp.broadcast_to(rows.reshape(2, 1, 6, 1), (2, 4, 6, 6)).reshape(2, CELLS)


def body(inputs, target, norm_gain_vector, w_qkv, w_proj, lat_region, lat_valid):
    strips = lax.axis_size("lon")
    mine = lax.axis_index("mem")
    place = place_matrix()
    start = mine * 12
    target_rows = lax.dynamic_slice_in_dim(target, start, 12, axis=1)
    packed, target_packed = pack(inputs, target_rows, jnp.asarray(place, BF))

    region = cell_rows(lax.dynamic_slice_in_dim(lat_region, start, 12))
    valid = cell_rows(lax.dynamic_slice_in_dim(lat_valid, start, 12))
    same = region[:, :, None] == region[:, None, :]
    itself = np.eye(CELLS, dtype=bool)
    bias = jnp.where(same & ((valid[:, :, None] == 1) | itself[None]), 0.0, -1e30).astype(F32)
    valid_column = valid.astype(F32)[:, :, None]

    west = [(i, (i - 1) % strips) for i in range(strips)]
    east = [(i, (i + 1) % strips) for i in range(strips)]
    target_beyond = lax.ppermute(target_packed[0], "lon", west)
    arrived = lax.all_to_all(packed, "mem", 0, 0, tiled=False)
    beyond = lax.ppermute(arrived[:, 0], "lon", west)
    sent = main(
        arrived[:, 1], beyond, jnp.stack([target_packed[1], target_beyond]), bias, valid_column, norm_gain_vector, w_qkv, w_proj
    )
    back = lax.all_to_all(sent, "mem", 0, 0, tiled=False)
    west_half = lax.ppermute(back[:, PIECE : 2 * PIECE], "lon", east)
    part = jnp.sum(back[:, 2 * PIECE :].astype(F32), axis=0)
    bit = 1
    while bit < strips:
        part = part + lax.ppermute(part, "lon", [(i, i ^ bit) for i in range(strips)])
        bit *= 2
    high = part.astype(BF)
    low = (part - high.astype(F32))[32:48].astype(BF)
    full = jnp.concatenate([high, low], axis=0)
    shared = lax.all_to_all(
        jnp.broadcast_to(full[None], (M, GRAD_ROWS + 16, 128)), "mem", 0, 0, tiled=False
    ).astype(F32)
    grads = shared[:, :GRAD_ROWS].reshape(M * GRAD_ROWS, 128)
    extra = shared[M - 1, 32:48] + shared[M - 1, GRAD_ROWS:]
    grad_inputs = unpack(back[:, :PIECE], west_half, jnp.asarray(place.T, BF))

    count = M * 2 * 96 * 12 * strips
    scale = count ** (-0.5)
    rest = grads[768:864]
    qkv_sum = jnp.concatenate(
        [grads[i * C : (i + 1) * C] for i in range(4)]
        + [jnp.concatenate([rest[:, :64], rest[:, 64:]], axis=0)], axis=1
    )
    last = grads[1056:1152]
    proj_sum = jnp.concatenate(
        [grads[864:1056], jnp.concatenate([last[:, :64], last[:, 64:]], axis=0)], axis=1
    )
    gain_sum = extra[:2].reshape(256)[:C]
    loss = (extra[2, 0] + extra[2, 1]) / (count * C)
    return (grad_inputs, qkv_sum * scale, proj_sum * scale, gain_sum * scale, loss)


def solution(mesh):
    in_specs = (
        P("mem", None, None, "lon", None),
        P(None, None, "lon", None),
        P(),
        P(),
        P(),
        P(),
        P(),
    )
    out_specs = (P("mem", None, None, "lon", None), P(), P(), P(), P())
    return jax.shard_map(body, mesh=mesh, in_specs=in_specs, out_specs=out_specs, check_vma=False)
```

```python
import functools

import jax
import jax.numpy as jnp
import numpy as np
from jax import lax
from jax.experimental import pallas as pl
from jax.experimental.pallas import tpu as pltpu
from jax.sharding import PartitionSpec as P

HEADS = 6
SIZE = 32
SHIFT = 6
C = 192
CELLS = 144
HALF = 72
M = 8
EPS = 1e-05
DELTA_SQ = 0.0625
PIECE = 112
GRAD_ROWS = 80
LOW_ROWS = 16
BF = jnp.bfloat16
F32 = jnp.float32
VMEM_LIMIT = 40 * 1024 * 1024


def dot(left, right):
    return jnp.dot(left, right, preferred_element_type=F32)


def dot_t(left, right):
    return lax.dot_general(left, right, (((1,), (1,)), ((), ())), preferred_element_type=F32)


def identity(n):
    return (
        lax.broadcasted_iota(jnp.int32, (n, n), 0) == lax.broadcasted_iota(jnp.int32, (n, n), 1)
    ).astype(BF)


def pack_half(cells):
    rest = jnp.concatenate([cells[:, 128:], jnp.zeros((HALF, 64), F32)], axis=1)
    second = jnp.concatenate([rest[40:], jnp.zeros((8, 128), F32)], axis=0)
    return jnp.concatenate([cells[:, :128], rest[:40] + pltpu.roll(second, 64, 1)], axis=0)


def unpack_half(piece):
    rest = piece[HALF:]
    rest = jnp.concatenate([rest[:, :64], pltpu.roll(rest, 64, 1)[:32, :64]], axis=0)
    return jnp.concatenate([piece[:HALF], rest], axis=1)


TILES = ((0,), (0, 1), (0, 1), (1,))
FIRST = (0, 0, 1, 1)


def place_matrices():
    cell = np.arange(288)
    half, block, level, row, column = cell // 144, cell // 72 % 2, cell // 36 % 2, cell // 6 % 6, cell % 6
    out = np.zeros((4, 2, 2, 288, 192), np.float32)
    for i, first in enumerate(FIRST):
        lat = 12 * i + 6 * block + row
        out[i, lat // 16 - first, level, cell, (half * 6 + column) * 16 + lat % 16] = 1.0
    return out


def cell_parts():
    cell = lax.broadcasted_iota(jnp.int32, (CELLS, 1), 0)
    block = (cell >= 72).astype(jnp.int32)
    cell = cell - 72 * block
    level = (cell >= 36).astype(jnp.int32)
    cell = cell - 36 * level
    row = sum((cell >= 6 * k).astype(jnp.int32) for k in range(1, 6))
    return 6 * block + row, level, cell - 6 * row


def place_of(parts, i, first, level, s):
    row, its_level, column = parts
    lat = 12 * i + row - 16 * (first + s)
    return jnp.where((lat >= 0) & (lat < 16) & (its_level == level), column * 16 + lat, -1)


def gather_group(place, steps, tile):
    lane = lax.broadcasted_iota(jnp.int32, (CELLS, 96), 1)
    cells = None
    for s in steps:
        for level in range(2):
            part = dot((place(level, s) == lane).astype(F32).astype(BF), tile(level, s))
            cells = part if cells is None else cells + part
    return cells


def pack_kernel(at_ref, x_hbm, out_ref, x_ref, semaphore):
    copy = pltpu.make_async_copy(x_hbm.at[0, :, pl.ds(at_ref[0] * 6, 6)], x_ref, semaphore)
    copy.start()
    parts = cell_parts()
    copy.wait()
    for quad in range(2):
        for i in range(4):

            def tile(level, s):
                at = 16 * (3 * quad + FIRST[i] + s)
                return x_ref[level, :, at : at + 16, :].reshape(96, C)

            def place(level, s):
                return place_of(parts, i, FIRST[i], level, s)

            cells = gather_group(place, TILES[i], tile)
            for sub in range(2):
                out_ref[8 * quad + 2 * i + sub] = pack_half(cells[sub * HALF : (sub + 1) * HALF]).astype(BF)


def pack(half, inputs):
    return pl.pallas_call(
        pack_kernel,
        in_specs=[SCALARS, pl.BlockSpec(memory_space=pl.ANY)],
        out_specs=WHOLE,
        out_shape=jax.ShapeDtypeStruct((2 * M, PIECE, 128), BF),
        scratch_shapes=[pltpu.VMEM((2, 6, 96, C), BF), pltpu.SemaphoreType.DMA],
        compiler_params=PARAMS,
        name="pack_strip",
    )(half, inputs)


def pack_target_kernel(at_ref, t_ref, even_keep, even_send, odd_keep, odd_send):
    member, odd_strip = at_ref[0], at_ref[1] == 1
    i = member // 2
    first = jnp.where(i >= 2, 1, 0)
    second = member % 2 == 1
    parts = cell_parts()
    pieces = []
    for quad in range(2):
        for half in range(2):

            def tile(level, s):
                at = pl.multiple_of(16 * (3 * quad + first + s), 16)
                return t_ref[level, 6 * half : 6 * half + 6, pl.ds(at, 16), :].reshape(96, C)

            def place(level, s):
                return place_of(parts, i, first, level, s)

            cells = gather_group(place, (0, 1), tile)
            pieces.append(pack_half(jnp.where(second, cells[HALF:], cells[:HALF])))
    low_west, low_east, high_west, high_east = pieces
    even_keep[...] = jnp.where(odd_strip, high_west, low_east).astype(BF)
    even_send[...] = jnp.where(odd_strip, low_west, high_east).astype(BF)
    odd_keep[...] = jnp.where(odd_strip, low_east, high_west).astype(BF)
    odd_send[...] = jnp.where(odd_strip, high_east, low_west).astype(BF)


def pack_target(at, target):
    return pl.pallas_call(
        pack_target_kernel,
        in_specs=[SCALARS, WHOLE],
        out_specs=[WHOLE] * 4,
        out_shape=[jax.ShapeDtypeStruct((PIECE, 128), BF)] * 4,
        compiler_params=PARAMS,
        name="pack_target",
    )(at, target)


WHOLE = pl.BlockSpec(memory_space=pltpu.VMEM)
SCALARS = pl.BlockSpec(memory_space=pltpu.SMEM)
PARAMS = pltpu.CompilerParams(vmem_limit_bytes=VMEM_LIMIT)


def unpack_kernel(at_ref, even_ref, odd_ref, place_ref, out_ref):
    odd_strip = at_ref[1] == 1
    for quad in range(2):
        groups = []
        for i in range(4):
            wests, easts = [], []
            for sub in range(2):
                even = even_ref[8 * quad + 2 * i + sub].astype(F32)
                odd = odd_ref[8 * quad + 2 * i + sub, :PIECE].astype(F32)
                wests.append(unpack_half(jnp.where(odd_strip, even, odd)))
                easts.append(unpack_half(jnp.where(odd_strip, odd, even)))
            groups.append(jnp.concatenate(wests + easts, axis=0).astype(BF))
        for t in range(3):
            at = 16 * (3 * quad + t)
            for level in range(2):
                slab = None
                for i in range(4):
                    if t - FIRST[i] in TILES[i]:
                        part = dot(place_ref[i, t - FIRST[i], level], groups[i])
                        slab = part if slab is None else slab + part
                out_ref[0, level, :, at : at + 16, :] = slab.astype(BF).reshape(12, 16, C)


def unpack(at, even, odd, place_t):
    return pl.pallas_call(
        unpack_kernel,
        in_specs=[SCALARS, WHOLE, WHOLE, WHOLE],
        out_specs=WHOLE,
        out_shape=jax.ShapeDtypeStruct((1, 2, 12, 96, C), BF),
        compiler_params=PARAMS,
        name="unpack_strip",
    )(at, even, odd, place_t)


def split_low(total, copies):
    high = total.astype(BF)
    low = (total - high.astype(F32))[32 : 32 + LOW_ROWS].astype(BF)
    return jnp.broadcast_to(jnp.concatenate([high, low], axis=0)[None], (copies, GRAD_ROWS + LOW_ROWS, 128))


def first_sum_kernel(back_ref, out_ref):
    total = jnp.sum(back_ref[:, PIECE:].astype(F32), axis=0)
    out_ref[...] = split_low(total, out_ref.shape[0])


def second_sum_kernel(parts_ref, out_ref):
    total = jnp.sum(parts_ref[...].astype(F32), axis=0)
    low = jnp.concatenate(
        [jnp.zeros((32, 128), F32), total[GRAD_ROWS:], jnp.zeros((GRAD_ROWS - 32 - LOW_ROWS, 128), F32)], axis=0
    )
    out_ref[...] = split_low(total[:GRAD_ROWS] + low, out_ref.shape[0])


def finish_kernel(scale, per_score, grads_ref, qkv_out, proj_out, gain_out, loss_out):
    rows = grads_ref[:, :GRAD_ROWS].astype(F32).reshape(2 * M * GRAD_ROWS, 128) * scale
    for i in range(4):
        qkv_out[:, 128 * i : 128 * (i + 1)] = rows[i * C : (i + 1) * C]
    rest = rows[768:864]
    qkv_out[:, 512:] = jnp.concatenate([rest[:, :64], pltpu.roll(rest, 64, 1)[:, :64]], axis=0)
    rest = rows[1056:1152]
    proj_out[:, :128] = rows[864:1056]
    proj_out[:, 128:] = jnp.concatenate([rest[:, :64], pltpu.roll(rest, 64, 1)[:, :64]], axis=0)
    piece = 1152 // GRAD_ROWS
    extra = grads_ref[piece, 32 : 32 + LOW_ROWS].astype(F32) + grads_ref[piece, GRAD_ROWS:].astype(F32)
    gain_out[...] = jnp.concatenate([extra[0:1], extra[1:2, :64]], axis=1) * scale
    loss_out[...] = (extra[2:3, 0:1] + extra[2:3, 1:2]) * per_score


def small(kernel, name, out_shape, *args):
    return pl.pallas_call(
        kernel,
        in_specs=[WHOLE] * len(args),
        out_specs=jax.tree.map(lambda _: WHOLE, out_shape),
        out_shape=out_shape,
        compiler_params=PARAMS,
        name=name,
    )(*args)


def head_only(field, head):
    lane = lax.broadcasted_iota(jnp.int32, field.shape, 1)
    return jnp.where((lane >= head * SIZE) & (lane < (head + 1) * SIZE), field, jnp.zeros_like(field))


def main_kernel(
    at_ref, x_ref, tk_ref, tr_ref, bias_ref, valid_ref, gain_ref, wkv_ref, wqkv_ref, wqkvt_ref, wproj_ref, wprojt_ref,
    *refs,
):
    refs = list(refs)
    start = [refs.pop(0) for _ in range(4)] if len(refs) > 21 else None
    out_ref = refs.pop(0)
    (x_s, t_s, xhat_s, rstd_s, n_s, k_s, v_s, qkvt_s, attf_s, att_s, p_s, mixed_s, gat_s, tot_s, ds_s, grad_s) = refs[-16:]
    sqkv_s, sproj_s, sgain_s, score_s = refs[:-16]
    scale = SIZE ** (-0.5)
    to_exp2 = scale * 1.4426950408889634
    last = M - 1

    for member in range(M):
        x_s[member] = jnp.concatenate(
            [unpack_half(x_ref[member].astype(F32)), unpack_half(x_ref[M + member].astype(F32))], axis=0
        )
    kept = unpack_half(tk_ref[...].astype(F32))
    received = unpack_half(tr_ref[...].astype(F32))
    eastern = at_ref[0] == 1
    t_s[...] = jnp.concatenate(
        [jnp.where(eastern, received, kept), jnp.where(eastern, kept, received)], axis=0
    )


    def project_qkv(window):
        x = x_s[window]
        centred = x - jnp.mean(x, axis=1, keepdims=True)
        rstd = lax.rsqrt(jnp.mean(centred * centred, axis=1, keepdims=True) + EPS)
        xhat = centred * rstd
        xhat_s[window] = xhat
        rstd_s[window] = rstd
        normed = (xhat * gain_ref[...]).astype(BF)
        n_s[window] = normed
        kv = dot(normed, wkv_ref[...]).astype(BF)
        k_s[window] = kv[:, :C]
        v_s[window] = kv[:, C:]
        qkvt_s[window] = dot_t(wqkvt_ref[...], normed).astype(BF)

    def score_head(window, head):
        scores = dot(head_only(k_s[window], head), qkvt_s[window, :C])
        expo = jnp.exp2(scores * to_exp2 + bias_ref[...])
        p_s[window, head] = (expo * (1.0 / jnp.sum(expo, axis=0, keepdims=True))).astype(BF)

    def attend_head(window, head):
        at = slice(head * SIZE, (head + 1) * SIZE)
        attended = dot(qkvt_s[window, 2 * C + head * SIZE : 2 * C + (head + 1) * SIZE], p_s[window, head])
        attf_s[window, at] = attended
        att_s[window, at] = attended.astype(BF)

    def heads(*stages):
        for stage, window in stages:
            for head in range(HEADS):
                stage(window, head)

    def forward(step, carry):
        projt = dot(wprojt_ref[...], att_s[step]).astype(BF)
        heads((attend_head, jnp.minimum(step + 1, last)), (score_head, jnp.minimum(step + 2, last)))
        project_qkv(jnp.minimum(step + 3, last))
        mixed_s[step] = x_s[step] + dot_t(identity(CELLS), projt)
        return carry

    project_qkv(0)
    heads((score_head, 0))
    project_qkv(1)
    heads((attend_head, 0), (score_head, 1))
    project_qkv(2)
    lax.fori_loop(0, M, forward, 0)

    def crps(step, score):
        rows = pl.ds(pl.multiple_of(step * 8, 8), 8)
        valid = valid_ref[rows]
        target = t_s[rows]
        mixed = [mixed_s[m, rows] for m in range(M)]
        rounded = [value.astype(BF).astype(F32) for value in mixed]
        slopes = [None] * M
        pairs = None
        for m in range(M):
            for n in range(m + 1, M):
                diff = rounded[m] - rounded[n]
                square = diff * diff + DELTA_SQ
                inverse = lax.rsqrt(square)
                size = square * inverse
                slope = diff * inverse
                pairs = size if pairs is None else pairs + size
                slopes[m] = slope if slopes[m] is None else slopes[m] + slope
                slopes[n] = -slope if slopes[n] is None else slopes[n] - slope
        total = -(2.0 * pairs + M * DELTA_SQ**0.5) / (2.0 * M)
        for m in range(M):
            diff = mixed[m] - target
            square = diff * diff + DELTA_SQ
            inverse = lax.rsqrt(square)
            total = total + square * inverse
            mixed_s[m, rows] = valid * (diff * inverse - slopes[m] / M)
        return score + valid * total

    if start is None:
        sqkv_s[...] = jnp.zeros_like(sqkv_s)
        sproj_s[...] = jnp.zeros_like(sproj_s)
        sgain_s[...] = jnp.zeros_like(sgain_s)
        score_s[...] = jnp.zeros_like(score_s)
    else:
        for ref, begin in zip((sqkv_s, sproj_s, sgain_s, score_s), start):
            ref[...] = begin[...]
    score_s[...] = lax.fori_loop(0, 18, crps, score_s[...])

    def grad_attended(window):
        gat = dot_t(wproj_ref[...], mixed_s[window].astype(BF)).astype(BF)
        gat_s[window] = gat
        product = gat.astype(F32) * attf_s[window]
        for head in range(HEADS):
            tot_s[window, head] = jnp.sum(product[head * SIZE : (head + 1) * SIZE], axis=0, keepdims=True)

    def grad_score_head(window, head):
        grad_probs = dot(head_only(v_s[window], head), gat_s[window])
        ds_s[window % 4, head] = (grad_probs - tot_s[window, head]).astype(BF) * p_s[window, head]

    def grad_qkv_head(window, head):
        at = slice(head * SIZE, (head + 1) * SIZE)
        grad_scores = ds_s[window % 4, head]
        qt = qkvt_s[window, at]
        kt = qkvt_s[window, C + head * SIZE : C + (head + 1) * SIZE]
        grad_s[window, at] = (dot(kt, grad_scores) * scale).astype(BF)
        grad_s[window, C + head * SIZE : C + (head + 1) * SIZE] = (dot_t(qt, grad_scores) * scale).astype(BF)
        grad_s[window, 2 * C + head * SIZE : 2 * C + (head + 1) * SIZE] = dot_t(
            gat_s[window, at], p_s[window, head]
        ).astype(BF)

    def grad_norm(window, gbt):
        grad_normed = dot_t(identity(CELLS), gbt)
        xhat = xhat_s[window]
        sgain_s[...] += jnp.sum((grad_normed * xhat).reshape(18, 8, C), axis=0)
        scaled = grad_normed * gain_ref[...]
        first = jnp.mean(scaled, axis=1, keepdims=True)
        second = jnp.mean(scaled * xhat, axis=1, keepdims=True)
        x_s[window] = mixed_s[window] + rstd_s[window] * (scaled - first - xhat * second)

    def backward(step, carry):
        gbt = dot(wqkv_ref[...], grad_s[step]).astype(BF)
        sqkv_s[...] += dot(grad_s[step], n_s[step])
        sproj_s[...] += dot(att_s[step], mixed_s[step].astype(BF))
        heads((grad_qkv_head, jnp.minimum(step + 1, last)), (grad_score_head, jnp.minimum(step + 2, last)))
        grad_attended(jnp.minimum(step + 3, last))
        grad_norm(step, gbt)
        return carry

    grad_attended(0)
    heads((grad_score_head, 0))
    grad_attended(1)
    heads((grad_qkv_head, 0), (grad_score_head, 1))
    grad_attended(2)
    lax.fori_loop(0, M, backward, 0)

    def pieces(member):
        return [pack_half(x_s[member, half * HALF : (half + 1) * HALF]).astype(BF) for half in range(2)]

    if start is None:
        for member in range(M):
            for half, piece in enumerate(pieces(member)):
                out_ref[half * M + member] = piece
        return

    sqkv = dot_t(identity(C), sqkv_s[...].astype(BF))
    sproj = sproj_s[...]
    pad = jnp.zeros((C, 64), F32)
    rest = jnp.concatenate([sqkv[:, 512:], pad], axis=1)
    rest = rest[:96] + pltpu.roll(rest[96:], 64, 1)
    proj_rest = jnp.concatenate([sproj[:, 128:], pad], axis=1)
    proj_rest = proj_rest[:96] + pltpu.roll(proj_rest[96:], 64, 1)
    sgain = jnp.sum(sgain_s[...], axis=0, keepdims=True)
    total = jnp.sum(jnp.sum(score_s[...], axis=0, keepdims=True), axis=1, keepdims=True)
    high = total.astype(BF).astype(F32)
    low = (total - high).astype(BF).astype(F32)
    row = lax.broadcasted_iota(jnp.int32, (128, 128), 0)
    lane = lax.broadcasted_iota(jnp.int32, (128, 128), 1)
    extra = jnp.where(row == 0, jnp.broadcast_to(sgain[:, :128], (128, 128)), 0.0)
    wide = jnp.concatenate([sgain[:, 128:], jnp.zeros((1, 64), F32)], axis=1)
    extra = extra + jnp.where(row == 1, jnp.broadcast_to(wide, (128, 128)), 0.0)
    extra = extra + jnp.where((row == 2) & (lane == 0), jnp.broadcast_to(high, (128, 128)), 0.0)
    extra = extra + jnp.where((row == 2) & (lane == 1), jnp.broadcast_to(low, (128, 128)), 0.0)
    grads = jnp.concatenate(
        [sqkv[:, 128 * i : 128 * (i + 1)] for i in range(4)] + [rest, sproj[:, :128], proj_rest, extra], axis=0
    ).astype(BF)
    for member in range(M):
        for half, piece in enumerate(pieces(member)):
            to = half * M + member
            out_ref[to] = jnp.concatenate([piece, grads[to * GRAD_ROWS : (to + 1) * GRAD_ROWS]], axis=0)


SUMS = [(3 * C, C), (C, C), (8, C), (8, C)]


def main(at, pieces, target_kept, target_received, bias, valid, gain, w_qkv, w_proj, sums=()):
    total = [jax.ShapeDtypeStruct(shape, F32) for shape in SUMS]
    rows = PIECE + GRAD_ROWS if sums else PIECE
    out = jax.ShapeDtypeStruct((2 * M, rows, 128), BF)
    scratch = [
        pltpu.VMEM((M, CELLS, C), F32),
        pltpu.VMEM((CELLS, C), F32),
        pltpu.VMEM((M, CELLS, C), F32),
        pltpu.VMEM((M, CELLS, 1), F32),
        pltpu.VMEM((M, CELLS, C), BF),
        pltpu.VMEM((M, CELLS, C), BF),
        pltpu.VMEM((M, CELLS, C), BF),
        pltpu.VMEM((M, 3 * C, CELLS), BF),
        pltpu.VMEM((M, C, CELLS), F32),
        pltpu.VMEM((M, C, CELLS), BF),
        pltpu.VMEM((M, HEADS, CELLS, CELLS), BF),
        pltpu.VMEM((M, CELLS, C), F32),
        pltpu.VMEM((M, C, CELLS), BF),
        pltpu.VMEM((M, HEADS, 1, CELLS), F32),
        pltpu.VMEM((4, HEADS, CELLS, CELLS), BF),
        pltpu.VMEM((M, 3 * C, CELLS), BF),
    ]
    if sums:
        scratch = [pltpu.VMEM(shape, F32) for shape in SUMS] + scratch
    args = (at, pieces, target_kept, target_received, bias, valid, gain[None], w_qkv[:, C:], w_qkv, w_qkv.T, w_proj, w_proj.T) + tuple(sums)
    return pl.pallas_call(
        main_kernel,
        in_specs=[SCALARS] + [WHOLE] * (len(args) - 1),
        out_specs=WHOLE if sums else [WHOLE] * 5,
        out_shape=out if sums else [out] + total,
        scratch_shapes=scratch,
        compiler_params=PARAMS,
        name="window_attention_crps",
    )(*args)


def body(inputs, target, norm_gain_vector, w_qkv, w_proj, lat_region, lat_valid):
    strips = lax.axis_size("lon")
    strip, member = lax.axis_index("lon"), lax.axis_index("mem")
    both = ("lon", "mem")

    def group(*members_of):
        return [strip * M + m for strip in members_of for m in range(M)]

    even_groups = [group(p, p + 1) for p in range(0, strips, 2)]
    odd_groups = [group(p + 1, (p + 2) % strips) for p in range(0, strips, 2)]
    alike_groups = [[(p + side) * M + m for p in range(0, strips, 2)] for side in range(2) for m in range(M)]
    even_swap = [(i, i ^ 1) for i in range(strips)]
    odd_swap = [(i, (i + 1 if i % 2 else i - 1) % strips) for i in range(strips)]

    def exchange(array, groups):
        return lax.all_to_all(array, both, 0, 0, axis_index_groups=groups)

    parity = strip % 2
    at = jnp.stack([member, parity]).astype(jnp.int32)
    side = parity.astype(jnp.int32)
    by_column = inputs.transpose(0, 1, 3, 2, 4)
    even = pack((1 - side)[None], by_column)
    odd = pack(side[None], by_column)
    even_keep, even_send, odd_keep, odd_send = pack_target(at, target.transpose(0, 2, 1, 3))
    even = exchange(even, even_groups)
    odd = exchange(odd, odd_groups)
    even_received = lax.ppermute(even_send, "lon", even_swap)
    odd_received = lax.ppermute(odd_send, "lon", odd_swap)
    even, even_received, odd_received = lax.optimization_barrier((even, even_received, odd_received))

    def of_block(side):
        first = (side * M + member) * 6
        region, valid = (
            jnp.broadcast_to(lax.dynamic_slice_in_dim(rows, first, 6).reshape(1, 6, 1), (4, 6, 6)).reshape(CELLS)
            for rows in (lat_region, lat_valid)
        )
        allowed = (region[:, None] == region[None, :]) & ((valid[:, None] == 1) | np.eye(CELLS, dtype=bool))
        return jnp.where(allowed, 0.0, -1e30).astype(F32), valid.astype(F32)[:, None]

    weights = (norm_gain_vector, w_qkv, w_proj)
    even_back, *sums = main(side[None], even, even_keep, even_received, *of_block(side), *weights)
    odd_back = main((1 - side)[None], odd, odd_keep, odd_received, *of_block(1 - side), *weights, sums=tuple(sums))
    even_back, odd_back = lax.optimization_barrier((exchange(even_back, even_groups), odd_back))
    odd_back = exchange(odd_back, odd_groups)

    count = M * 2 * 96 * 12 * strips
    rows = GRAD_ROWS + LOW_ROWS
    part = small(first_sum_kernel, "sum_group", jax.ShapeDtypeStruct((strips // 2, rows, 128), BF), odd_back)
    part = exchange(part, alike_groups)
    part = small(second_sum_kernel, "sum_all", jax.ShapeDtypeStruct((2 * M, rows, 128), BF), part)
    part = exchange(part, odd_groups)
    grad_inputs = unpack(at, even_back, odd_back, jnp.asarray(place_matrices().swapaxes(3, 4), BF)).transpose(0, 1, 3, 2, 4)
    grad_qkv, grad_proj, grad_gain, loss = small(
        functools.partial(finish_kernel, count ** (-0.5), 1.0 / (count * C)),
        "finish",
        [jax.ShapeDtypeStruct(shape, F32) for shape in ((C, 3 * C), (C, C), (1, C), (1, 1))],
        part,
    )
    return (grad_inputs, grad_qkv, grad_proj, grad_gain[0], loss[0, 0])


def solution(mesh):
    in_specs = (
        P("mem", None, None, "lon", None),
        P(None, None, "lon", None),
        P(),
        P(),
        P(),
        P(),
        P(),
    )
    out_specs = (P("mem", None, None, "lon", None), P(), P(), P(), P())
    return jax.shard_map(body, mesh=mesh, in_specs=in_specs, out_specs=out_specs, check_vma=False)
```

```python
import functools

import jax
import jax.numpy as jnp
import numpy as np
from jax import lax
from jax.experimental import pallas as pl
from jax.experimental.pallas import tpu as pltpu
from jax.sharding import PartitionSpec as P

HEADS = 6
SIZE = 32
SHIFT = 6
C = 192
CELLS = 144
HALF = 72
M = 8
EPS = 1e-05
DELTA_SQ = 0.0625
PIECE = 112
GRAD_ROWS = 80
LOW_ROWS = 16
BF = jnp.bfloat16
F32 = jnp.float32
VMEM_LIMIT = 40 * 1024 * 1024


def dot(left, right):
    return jnp.dot(left, right, preferred_element_type=F32)


def dot_t(left, right):
    return lax.dot_general(left, right, (((1,), (1,)), ((), ())), preferred_element_type=F32)


def identity(n):
    return (
        lax.broadcasted_iota(jnp.int32, (n, n), 0) == lax.broadcasted_iota(jnp.int32, (n, n), 1)
    ).astype(BF)


def pack_half(cells):
    rest = jnp.concatenate([cells[:, 128:], jnp.zeros((HALF, 64), F32)], axis=1)
    second = jnp.concatenate([rest[40:], jnp.zeros((8, 128), F32)], axis=0)
    return jnp.concatenate([cells[:, :128], rest[:40] + pltpu.roll(second, 64, 1)], axis=0)


def unpack_half(piece):
    rest = piece[HALF:]
    rest = jnp.concatenate([rest[:, :64], pltpu.roll(rest, 64, 1)[:32, :64]], axis=0)
    return jnp.concatenate([piece[:HALF], rest], axis=1)


TILES = ((0,), (0, 1), (0, 1), (1,))
FIRST = (0, 0, 1, 1)


def cell_parts(axis):
    cell = lax.broadcasted_iota(jnp.int32, (CELLS, 1) if axis == 0 else (1, CELLS), axis)
    block = (cell >= 72).astype(jnp.int32)
    cell = cell - 72 * block
    level = (cell >= 36).astype(jnp.int32)
    cell = cell - 36 * level
    row = sum((cell >= 6 * k).astype(jnp.int32) for k in range(1, 6))
    return 6 * block + row, level, cell - 6 * row


def place_of(parts, i, first, level, s):
    row, its_level, column = parts
    lat = 12 * i + row - 16 * (first + s)
    return jnp.where((lat >= 0) & (lat < 16) & (its_level == level), column * 16 + lat, -1)


def gather_group(place, steps, tile):
    lane = lax.broadcasted_iota(jnp.int32, (CELLS, 96), 1)
    cells = None
    for s in steps:
        for level in range(2):
            part = dot((place(level, s) == lane).astype(F32).astype(BF), tile(level, s))
            cells = part if cells is None else cells + part
    return cells


def pack_kernel(at_ref, x_hbm, out_ref, x_ref, semaphore):
    copy = pltpu.make_async_copy(x_hbm.at[0, :, pl.ds(at_ref[0] * 6, 6)], x_ref, semaphore)
    copy.start()
    parts = cell_parts(0)
    copy.wait()
    for quad in range(2):
        for i in range(4):

            def tile(level, s):
                at = 16 * (3 * quad + FIRST[i] + s)
                return x_ref[level, :, at : at + 16, :].reshape(96, C)

            def place(level, s):
                return place_of(parts, i, FIRST[i], level, s)

            cells = gather_group(place, TILES[i], tile)
            for sub in range(2):
                out_ref[8 * quad + 2 * i + sub] = pack_half(cells[sub * HALF : (sub + 1) * HALF]).astype(BF)


def pack(half, inputs):
    return pl.pallas_call(
        pack_kernel,
        in_specs=[SCALARS, HBM],
        out_specs=WHOLE,
        out_shape=jax.ShapeDtypeStruct((2 * M, PIECE, 128), BF),
        scratch_shapes=[pltpu.VMEM((2, 6, 96, C), BF), pltpu.SemaphoreType.DMA],
        compiler_params=PARAMS,
        name="pack_strip",
    )(half, inputs)


def pack_target_kernel(at_ref, t_ref, even_keep, even_send, odd_keep, odd_send):
    member, odd_strip = at_ref[0], at_ref[1] == 1
    i = member // 2
    first = jnp.where(i >= 2, 1, 0)
    second = member % 2 == 1
    parts = cell_parts(0)
    pieces = []
    for quad in range(2):
        for half in range(2):

            def tile(level, s):
                at = pl.multiple_of(16 * (3 * quad + first + s), 16)
                return t_ref[level, 6 * half : 6 * half + 6, pl.ds(at, 16), :].reshape(96, C)

            def place(level, s):
                return place_of(parts, i, first, level, s)

            cells = gather_group(place, (0, 1), tile)
            pieces.append(pack_half(jnp.where(second, cells[HALF:], cells[:HALF])))
    low_west, low_east, high_west, high_east = pieces
    even_keep[...] = jnp.where(odd_strip, high_west, low_east).astype(BF)
    even_send[...] = jnp.where(odd_strip, low_west, high_east).astype(BF)
    odd_keep[...] = jnp.where(odd_strip, low_east, high_west).astype(BF)
    odd_send[...] = jnp.where(odd_strip, high_east, low_west).astype(BF)


def pack_target(at, target):
    return pl.pallas_call(
        pack_target_kernel,
        in_specs=[SCALARS, WHOLE],
        out_specs=[WHOLE] * 4,
        out_shape=[jax.ShapeDtypeStruct((PIECE, 128), BF)] * 4,
        compiler_params=PARAMS,
        name="pack_target",
    )(at, target)


WHOLE = pl.BlockSpec(memory_space=pltpu.VMEM)
SCALARS = pl.BlockSpec(memory_space=pltpu.SMEM)
HBM = pl.BlockSpec(memory_space=pltpu.HBM)
PARAMS = pltpu.CompilerParams(vmem_limit_bytes=VMEM_LIMIT)


def unpack_half_strip(half, back_ref, out_hbm, cells_s, slabs_s, semaphore):
    parts = cell_parts(1)
    slot = lax.broadcasted_iota(jnp.int32, (96, CELLS), 0)
    for block in range(2 * M):
        cells_s[block // 2, block % 2 * HALF : (block % 2 + 1) * HALF] = unpack_half(back_ref[block, :PIECE].astype(F32))
    for quad in range(2):
        groups = [cells_s[4 * quad + i].astype(BF) for i in range(4)]
        for t in range(3):
            at = 16 * (3 * quad + t)
            for level in range(2):
                slab = None
                for i in range(4):
                    if t - FIRST[i] in TILES[i]:
                        place = (place_of(parts, i, t, level, 0) == slot).astype(F32).astype(BF)
                        part = dot(place, groups[i])
                        slab = part if slab is None else slab + part
                slabs_s[level, :, at : at + 16, :] = slab.astype(BF).reshape(6, 16, C)
    copy = pltpu.make_async_copy(slabs_s, out_hbm.at[0, :, pl.ds(half * 6, 6)], semaphore)
    copy.start()
    return copy


UNPACK_SCRATCH = [
    pltpu.VMEM((M, CELLS, C), F32),
    pltpu.VMEM((2, 6, 96, C), BF),
    pltpu.SemaphoreType.DMA,
]
STRIP = jax.ShapeDtypeStruct((1, 2, 12, 96, C), BF)


def unpack_kernel(half_ref, back_ref, out_hbm, *scratch):
    unpack_half_strip(half_ref[0], back_ref, out_hbm, *scratch).wait()


def unpack(half, back):
    return pl.pallas_call(
        unpack_kernel,
        in_specs=[SCALARS, WHOLE],
        out_specs=HBM,
        out_shape=STRIP,
        scratch_shapes=UNPACK_SCRATCH,
        compiler_params=PARAMS,
        name="unpack_strip",
    )(half, back)


def split_low(total, copies):
    high = total.astype(BF)
    low = (total - high.astype(F32))[32 : 32 + LOW_ROWS].astype(BF)
    return jnp.broadcast_to(jnp.concatenate([high, low], axis=0)[None], (copies, GRAD_ROWS + LOW_ROWS, 128))


def first_sum_kernel(back_ref, out_ref):
    total = jnp.sum(back_ref[:, PIECE:].astype(F32), axis=0)
    out_ref[...] = split_low(total, out_ref.shape[0])


def second_sum_kernel(parts_ref, back_ref, out_ref):
    total = jnp.sum(parts_ref[...].astype(F32), axis=0)
    low = jnp.concatenate(
        [jnp.zeros((32, 128), F32), total[GRAD_ROWS:], jnp.zeros((GRAD_ROWS - 32 - LOW_ROWS, 128), F32)], axis=0
    )
    out_ref[:, :PIECE] = back_ref[...]
    out_ref[:, PIECE:] = split_low(total[:GRAD_ROWS] + low, out_ref.shape[0])


def finish_kernel(
    scale, per_score, half_ref, back_ref, half_done, out_hbm, qkv_out, proj_out, gain_out, loss_out, *scratch
):
    del half_done
    copy = unpack_half_strip(half_ref[0], back_ref, out_hbm, *scratch)
    pieces = [back_ref[(i + M) % (2 * M), PIECE : PIECE + GRAD_ROWS] for i in range(2 * M)]
    rows = jnp.concatenate(pieces, axis=0).astype(F32) * scale
    for i in range(4):
        qkv_out[:, 128 * i : 128 * (i + 1)] = rows[i * C : (i + 1) * C]
    rest = rows[768:864]
    qkv_out[:, 512:] = jnp.concatenate([rest[:, :64], pltpu.roll(rest, 64, 1)[:, :64]], axis=0)
    rest = rows[1056:1152]
    proj_out[:, :128] = rows[864:1056]
    proj_out[:, 128:] = jnp.concatenate([rest[:, :64], pltpu.roll(rest, 64, 1)[:, :64]], axis=0)
    piece = (1152 // GRAD_ROWS + M) % (2 * M)
    at = PIECE + 32
    extra = back_ref[piece, at : at + LOW_ROWS].astype(F32) + back_ref[piece, PIECE + GRAD_ROWS :].astype(F32)
    gain_out[...] = jnp.concatenate([extra[0:1], extra[1:2, :64]], axis=1) * scale
    loss_out[...] = (extra[2:3, 0:1] + extra[2:3, 1:2]) * per_score
    copy.wait()


def finish(half, back, half_done, count):
    return pl.pallas_call(
        functools.partial(finish_kernel, count ** (-0.5), 1.0 / (count * C)),
        in_specs=[SCALARS, WHOLE, HBM],
        out_specs=[HBM] + [WHOLE] * 4,
        out_shape=[STRIP] + [jax.ShapeDtypeStruct(shape, F32) for shape in ((C, 3 * C), (C, C), (1, C), (1, 1))],
        scratch_shapes=UNPACK_SCRATCH,
        input_output_aliases={2: 0},
        compiler_params=PARAMS,
        name="finish",
    )(half, back, half_done)


def small(kernel, name, out_shape, *args):
    return pl.pallas_call(
        kernel,
        in_specs=[WHOLE] * len(args),
        out_specs=jax.tree.map(lambda _: WHOLE, out_shape),
        out_shape=out_shape,
        compiler_params=PARAMS,
        name=name,
    )(*args)


def head_only(field, head):
    lane = lax.broadcasted_iota(jnp.int32, field.shape, 1)
    return jnp.where((lane >= head * SIZE) & (lane < (head + 1) * SIZE), field, jnp.zeros_like(field))


def main_kernel(
    at_ref, x_ref, t_ref, aux_ref, bias_ref, wkv_ref, wqkv_ref, wqkvt_ref, wproj_ref, wprojt_ref, *refs
):
    refs = list(refs)
    before_ref = refs.pop(0) if len(refs) > 18 else None
    out_ref, sums_s = refs[:2]
    (x_s, t_s, xhat_s, rstd_s, n_s, k_s, v_s, qkvt_s, attf_s, att_s, p_s, mixed_s, gat_s, tot_s, ds_s, grad_s) = refs[2:]
    sqkv_s, sproj_s, sgain_s, score_s = (
        sums_s.at[start : start + rows] for start, rows in ((0, 3 * C), (3 * C, C), (4 * C, 8), (4 * C + 8, 8))
    )
    gain_ref, valid_ref = aux_ref.at[CELLS : CELLS + 1], aux_ref.at[:CELLS]
    scale = SIZE ** (-0.5)
    to_exp2 = scale * 1.4426950408889634
    last = M - 1

    for member in range(M):
        x_s[member] = jnp.concatenate(
            [unpack_half(x_ref[member].astype(F32)), unpack_half(x_ref[M + member].astype(F32))], axis=0
        )
    kept = unpack_half(t_ref[0].astype(F32))
    received = unpack_half(t_ref[1].astype(F32))
    eastern = at_ref[0] == 1
    t_s[...] = jnp.concatenate(
        [jnp.where(eastern, received, kept), jnp.where(eastern, kept, received)], axis=0
    )


    def project_qkv(window):
        x = x_s[window]
        centred = x - jnp.mean(x, axis=1, keepdims=True)
        rstd = lax.rsqrt(jnp.mean(centred * centred, axis=1, keepdims=True) + EPS)
        xhat = centred * rstd
        xhat_s[window] = xhat
        rstd_s[window] = rstd
        normed = (xhat * gain_ref[...]).astype(BF)
        n_s[window] = normed
        kv = dot(normed, wkv_ref[...]).astype(BF)
        k_s[window] = kv[:, :C]
        v_s[window] = kv[:, C:]
        qkvt_s[window] = dot_t(wqkvt_ref[...], normed).astype(BF)

    def score_head(window, head):
        scores = dot(head_only(k_s[window], head), qkvt_s[window, :C])
        expo = jnp.exp2(scores * to_exp2 + bias_ref[...])
        p_s[window, head] = (expo * (1.0 / jnp.sum(expo, axis=0, keepdims=True))).astype(BF)

    def attend_head(window, head):
        at = slice(head * SIZE, (head + 1) * SIZE)
        attended = dot(qkvt_s[window, 2 * C + head * SIZE : 2 * C + (head + 1) * SIZE], p_s[window, head])
        attf_s[window, at] = attended
        att_s[window, at] = attended.astype(BF)

    def heads(*stages):
        for stage, window in stages:
            for head in range(HEADS):
                stage(window, head)

    def forward(step, carry):
        projt = dot(wprojt_ref[...], att_s[step]).astype(BF)
        heads((attend_head, jnp.minimum(step + 1, last)), (score_head, jnp.minimum(step + 2, last)))
        project_qkv(jnp.minimum(step + 3, last))
        mixed_s[step] = x_s[step] + projt.T.astype(F32)
        return carry

    project_qkv(0)
    heads((score_head, 0))
    project_qkv(1)
    heads((attend_head, 0), (score_head, 1))
    project_qkv(2)
    lax.fori_loop(0, M, forward, 0)

    def crps(step, score):
        rows = pl.ds(pl.multiple_of(step * 8, 8), 8)
        valid = valid_ref[rows]
        target = t_s[rows]
        mixed = [mixed_s[m, rows] for m in range(M)]
        rounded = [value.astype(BF).astype(F32) for value in mixed]
        slopes = [None] * M
        pairs = None
        for m in range(M):
            for n in range(m + 1, M):
                diff = rounded[m] - rounded[n]
                square = diff * diff + DELTA_SQ
                inverse = lax.rsqrt(square)
                size = square * inverse
                slope = diff * inverse
                pairs = size if pairs is None else pairs + size
                slopes[m] = slope if slopes[m] is None else slopes[m] + slope
                slopes[n] = -slope if slopes[n] is None else slopes[n] - slope
        total = -(2.0 * pairs + M * DELTA_SQ**0.5) / (2.0 * M)
        for m in range(M):
            diff = mixed[m] - target
            square = diff * diff + DELTA_SQ
            inverse = lax.rsqrt(square)
            total = total + square * inverse
            mixed_s[m, rows] = valid * (diff * inverse - slopes[m] / M)
        return score + valid * total

    sums_s[...] = jnp.zeros_like(sums_s) if before_ref is None else before_ref[...]
    score_s[...] = lax.fori_loop(0, 18, crps, score_s[...])

    def grad_attended(window):
        gat = dot_t(wproj_ref[...], mixed_s[window].astype(BF)).astype(BF)
        gat_s[window] = gat
        product = gat.astype(F32) * attf_s[window]
        for head in range(HEADS):
            tot_s[window, head] = jnp.sum(product[head * SIZE : (head + 1) * SIZE], axis=0, keepdims=True)

    def grad_score_head(window, head):
        grad_probs = dot(head_only(v_s[window], head), gat_s[window])
        ds_s[window % 4, head] = (grad_probs - tot_s[window, head]).astype(BF) * p_s[window, head]

    def grad_qkv_head(window, head):
        at = slice(head * SIZE, (head + 1) * SIZE)
        grad_scores = ds_s[window % 4, head]
        qt = qkvt_s[window, at]
        kt = qkvt_s[window, C + head * SIZE : C + (head + 1) * SIZE]
        grad_s[window, at] = (dot(kt, grad_scores) * scale).astype(BF)
        grad_s[window, C + head * SIZE : C + (head + 1) * SIZE] = (dot_t(qt, grad_scores) * scale).astype(BF)
        grad_s[window, 2 * C + head * SIZE : 2 * C + (head + 1) * SIZE] = dot_t(
            gat_s[window, at], p_s[window, head]
        ).astype(BF)

    def grad_norm(window, gbt):
        grad_normed = gbt.T.astype(F32)
        xhat = xhat_s[window]
        sgain_s[...] += jnp.sum((grad_normed * xhat).reshape(18, 8, C), axis=0)
        scaled = grad_normed * gain_ref[...]
        first = jnp.mean(scaled, axis=1, keepdims=True)
        second = jnp.mean(scaled * xhat, axis=1, keepdims=True)
        x_s[window] = mixed_s[window] + rstd_s[window] * (scaled - first - xhat * second)

    def backward(step, carry):
        gbt = dot(wqkv_ref[...], grad_s[step]).astype(BF)
        sqkv_s[...] += dot(grad_s[step], n_s[step])
        sproj_s[...] += dot(att_s[step], mixed_s[step].astype(BF))
        heads((grad_qkv_head, jnp.minimum(step + 1, last)), (grad_score_head, jnp.minimum(step + 2, last)))
        grad_attended(jnp.minimum(step + 3, last))
        grad_norm(step, gbt)
        return carry

    grad_attended(0)
    heads((grad_score_head, 0))
    grad_attended(1)
    heads((grad_qkv_head, 0), (grad_score_head, 1))
    grad_attended(2)
    lax.fori_loop(0, M, backward, 0, unroll=2)

    def pieces(member):
        return [pack_half(x_s[member, half * HALF : (half + 1) * HALF]).astype(BF) for half in range(2)]

    if before_ref is None:
        for member in range(M):
            for half, piece in enumerate(pieces(member)):
                out_ref[half * M + member] = piece
        return

    sqkv = dot_t(identity(C), sqkv_s[...].astype(BF))
    sproj = sproj_s[...]
    pad = jnp.zeros((C, 64), F32)
    rest = jnp.concatenate([sqkv[:, 512:], pad], axis=1)
    rest = rest[:96] + pltpu.roll(rest[96:], 64, 1)
    proj_rest = jnp.concatenate([sproj[:, 128:], pad], axis=1)
    proj_rest = proj_rest[:96] + pltpu.roll(proj_rest[96:], 64, 1)
    sgain = jnp.sum(sgain_s[...], axis=0, keepdims=True)
    total = jnp.sum(jnp.sum(score_s[...], axis=0, keepdims=True), axis=1, keepdims=True)
    high = total.astype(BF).astype(F32)
    low = (total - high).astype(BF).astype(F32)
    row = lax.broadcasted_iota(jnp.int32, (128, 128), 0)
    lane = lax.broadcasted_iota(jnp.int32, (128, 128), 1)
    extra = jnp.where(row == 0, jnp.broadcast_to(sgain[:, :128], (128, 128)), 0.0)
    wide = jnp.concatenate([sgain[:, 128:], jnp.zeros((1, 64), F32)], axis=1)
    extra = extra + jnp.where(row == 1, jnp.broadcast_to(wide, (128, 128)), 0.0)
    extra = extra + jnp.where((row == 2) & (lane == 0), jnp.broadcast_to(high, (128, 128)), 0.0)
    extra = extra + jnp.where((row == 2) & (lane == 1), jnp.broadcast_to(low, (128, 128)), 0.0)
    grads = jnp.concatenate(
        [sqkv[:, 128 * i : 128 * (i + 1)] for i in range(4)] + [rest, sproj[:, :128], proj_rest, extra], axis=0
    ).astype(BF)
    for member in range(M):
        for half, piece in enumerate(pieces(member)):
            to = half * M + member
            out_ref[to] = jnp.concatenate([piece, grads[to * GRAD_ROWS : (to + 1) * GRAD_ROWS]], axis=0)


SUMS = (4 * C + 16, C)


def main(at, pieces, target, aux, bias, weights, before=None):
    sums = jax.ShapeDtypeStruct(SUMS, F32)
    out = jax.ShapeDtypeStruct((2 * M, PIECE if before is None else PIECE + GRAD_ROWS, 128), BF)
    scratch = [
        pltpu.VMEM((M, CELLS, C), F32),
        pltpu.VMEM((CELLS, C), F32),
        pltpu.VMEM((M, CELLS, C), F32),
        pltpu.VMEM((M, CELLS, 1), F32),
        pltpu.VMEM((M, CELLS, C), BF),
        pltpu.VMEM((M, CELLS, C), BF),
        pltpu.VMEM((M, CELLS, C), BF),
        pltpu.VMEM((M, 3 * C, CELLS), BF),
        pltpu.VMEM((M, C, CELLS), F32),
        pltpu.VMEM((M, C, CELLS), BF),
        pltpu.VMEM((M, HEADS, CELLS, CELLS), BF),
        pltpu.VMEM((M, CELLS, C), F32),
        pltpu.VMEM((M, C, CELLS), BF),
        pltpu.VMEM((M, HEADS, 1, CELLS), F32),
        pltpu.VMEM((4, HEADS, CELLS, CELLS), BF),
        pltpu.VMEM((M, 3 * C, CELLS), BF),
    ]
    args = (at, pieces, target, aux, bias) + tuple(weights)
    if before is not None:
        scratch = [pltpu.VMEM(SUMS, F32)] + scratch
        args += (before,)
    return pl.pallas_call(
        main_kernel,
        in_specs=[SCALARS] + [WHOLE] * (len(args) - 1),
        out_specs=[WHOLE] * 2 if before is None else WHOLE,
        out_shape=[out, sums] if before is None else out,
        scratch_shapes=scratch,
        compiler_params=PARAMS,
        name="window_attention_crps",
    )(*args)


def body(inputs, target, norm_gain_vector, w_qkv, w_proj, lat_region, lat_valid):
    strips = lax.axis_size("lon")
    strip, member = lax.axis_index("lon"), lax.axis_index("mem")
    both = ("lon", "mem")

    def group(*members_of):
        return [strip * M + m for strip in members_of for m in range(M)]

    even_groups = [group(p, p + 1) for p in range(0, strips, 2)]
    odd_groups = [group(p + 1, (p + 2) % strips) for p in range(0, strips, 2)]
    alike_groups = [[(p + side) * M + m for p in range(0, strips, 2)] for side in range(2) for m in range(M)]
    even_swap = [(i, i ^ 1) for i in range(strips)]
    odd_swap = [(i, (i + 1 if i % 2 else i - 1) % strips) for i in range(strips)]

    def exchange(array, groups):
        return lax.all_to_all(array, both, 0, 0, axis_index_groups=groups)

    parity = strip % 2
    at = jnp.stack([member, parity]).astype(jnp.int32)
    side = parity.astype(jnp.int32)
    by_column = inputs.transpose(0, 1, 3, 2, 4)
    even = pack((1 - side)[None], by_column)
    even, target, by_column = lax.optimization_barrier((even, target, by_column))
    odd = pack(side[None], by_column)
    even_keep, even_send, odd_keep, odd_send = pack_target(at, target.transpose(0, 2, 1, 3))
    even = exchange(even, even_groups)
    even_target = jnp.stack([even_keep, lax.ppermute(even_send, "lon", even_swap)])
    odd_target = jnp.stack([odd_keep, lax.ppermute(odd_send, "lon", odd_swap)])

    def of_block(side):
        first = (side * M + member) * 6
        region, valid = (
            jnp.broadcast_to(lax.dynamic_slice_in_dim(rows, first, 6).reshape(1, 6, 1), (4, 6, 6)).reshape(CELLS)
            for rows in (lat_region, lat_valid)
        )
        allowed = (region[:, None] == region[None, :]) & ((valid[:, None] == 1) | np.eye(CELLS, dtype=bool))
        aux = jnp.concatenate(
            [jnp.broadcast_to(valid.astype(F32)[:, None], (CELLS, C)), jnp.broadcast_to(norm_gain_vector[None], (8, C))]
        )
        return aux, jnp.where(allowed, 0.0, -1e30).astype(F32)

    even_extra, odd_extra = (even_target, *of_block(side)), (odd_target, *of_block(1 - side))
    weights = (w_qkv[:, C:], w_qkv, w_qkv.T, w_proj, w_proj.T)
    odd, even_extra, odd_extra, weights = lax.optimization_barrier((odd, even_extra, odd_extra, weights))
    odd = exchange(odd, odd_groups)
    even_back, sums = main(side[None], even, *even_extra, weights)
    odd_back = main((1 - side)[None], odd, *odd_extra, weights, sums)
    odd_back = exchange(odd_back, odd_groups)

    count = M * 2 * 96 * 12 * strips
    rows = GRAD_ROWS + LOW_ROWS
    part = small(first_sum_kernel, "sum_group", jax.ShapeDtypeStruct((strips // 2, rows, 128), BF), odd_back)
    part = exchange(part, alike_groups)
    last = jax.ShapeDtypeStruct((2 * M, PIECE + rows, 128), BF)
    back = exchange(small(second_sum_kernel, "sum_all", last, part, even_back), even_groups)
    half_done = unpack(side[None], odd_back)
    by_column, grad_qkv, grad_proj, grad_gain, loss = finish((1 - side)[None], back, half_done, count)
    grad_inputs = by_column.transpose(0, 1, 3, 2, 4)
    return (grad_inputs, grad_qkv, grad_proj, grad_gain[0], loss[0, 0])


def solution(mesh):
    in_specs = (
        P("mem", None, None, "lon", None),
        P(None, None, "lon", None),
        P(),
        P(),
        P(),
        P(),
        P(),
    )
    out_specs = (P("mem", None, None, "lon", None), P(), P(), P(), P())
    return jax.shard_map(body, mesh=mesh, in_specs=in_specs, out_specs=out_specs, check_vma=False)
```

```python
import functools

import jax
import jax.numpy as jnp
import numpy as np
from jax import lax
from jax.experimental import pallas as pl
from jax.experimental.pallas import tpu as pltpu
from jax.sharding import PartitionSpec as P

HEADS = 6
SIZE = 32
SHIFT = 6
C = 192
CELLS = 144
HALF = 72
M = 8
EPS = 1e-05
DELTA_SQ = 0.0625
PIECE = 112
GRAD_ROWS = 80
LOW_ROWS = 16
BF = jnp.bfloat16
F32 = jnp.float32
VMEM_LIMIT = 40 * 1024 * 1024


def dot(left, right):
    return jnp.dot(left, right, preferred_element_type=F32)


def dot_t(left, right):
    return lax.dot_general(left, right, (((1,), (1,)), ((), ())), preferred_element_type=F32)


def identity(n):
    return (
        lax.broadcasted_iota(jnp.int32, (n, n), 0) == lax.broadcasted_iota(jnp.int32, (n, n), 1)
    ).astype(BF)


def pack_half(cells):
    rest = jnp.concatenate([cells[:, 128:], jnp.zeros((HALF, 64), F32)], axis=1)
    second = jnp.concatenate([rest[40:], jnp.zeros((8, 128), F32)], axis=0)
    return jnp.concatenate([cells[:, :128], rest[:40] + pltpu.roll(second, 64, 1)], axis=0)


def unpack_half(piece):
    rest = piece[HALF:]
    rest = jnp.concatenate([rest[:, :64], pltpu.roll(rest, 64, 1)[:32, :64]], axis=0)
    return jnp.concatenate([piece[:HALF], rest], axis=1)


TILES = ((0,), (0, 1), (0, 1), (1,))
FIRST = (0, 0, 1, 1)


def cell_parts(axis):
    cell = lax.broadcasted_iota(jnp.int32, (CELLS, 1) if axis == 0 else (1, CELLS), axis)
    block = (cell >= 72).astype(jnp.int32)
    cell = cell - 72 * block
    level = (cell >= 36).astype(jnp.int32)
    cell = cell - 36 * level
    row = sum((cell >= 6 * k).astype(jnp.int32) for k in range(1, 6))
    return 6 * block + row, level, cell - 6 * row


def place_of(parts, i, first, level, s):
    row, its_level, column = parts
    lat = 12 * i + row - 16 * (first + s)
    return jnp.where((lat >= 0) & (lat < 16) & (its_level == level), column * 16 + lat, -1)


def gather_group(place, steps, tile):
    lane = lax.broadcasted_iota(jnp.int32, (CELLS, 96), 1)
    cells = None
    for s in steps:
        for level in range(2):
            part = dot((place(level, s) == lane).astype(F32).astype(BF), tile(level, s))
            cells = part if cells is None else cells + part
    return cells


def pack_kernel(at_ref, x_hbm, out_ref, x_ref, semaphore):
    copy = pltpu.make_async_copy(x_hbm.at[0, :, pl.ds(at_ref[0] * 6, 6)], x_ref, semaphore)
    copy.start()
    parts = cell_parts(0)
    copy.wait()
    for quad in range(2):
        for i in range(4):

            def tile(level, s):
                at = 16 * (3 * quad + FIRST[i] + s)
                return x_ref[level, :, at : at + 16, :].reshape(96, C)

            def place(level, s):
                return place_of(parts, i, FIRST[i], level, s)

            cells = gather_group(place, TILES[i], tile)
            for sub in range(2):
                out_ref[8 * quad + 2 * i + sub] = pack_half(cells[sub * HALF : (sub + 1) * HALF]).astype(BF)


def pack(half, inputs):
    return pl.pallas_call(
        pack_kernel,
        in_specs=[SCALARS, HBM],
        out_specs=WHOLE,
        out_shape=jax.ShapeDtypeStruct((2 * M, PIECE, 128), BF),
        scratch_shapes=[pltpu.VMEM((2, 6, 96, C), BF), pltpu.SemaphoreType.DMA],
        compiler_params=PARAMS,
        name="pack_strip",
    )(half, inputs)


def pack_target_kernel(at_ref, t_ref, even_keep, even_send, odd_keep, odd_send):
    member, odd_strip = at_ref[0], at_ref[1] == 1
    i = member // 2
    first = jnp.where(i >= 2, 1, 0)
    second = member % 2 == 1
    parts = cell_parts(0)
    pieces = []
    for quad in range(2):
        for half in range(2):

            def tile(level, s):
                at = pl.multiple_of(16 * (3 * quad + first + s), 16)
                return t_ref[level, 6 * half : 6 * half + 6, pl.ds(at, 16), :].reshape(96, C)

            def place(level, s):
                return place_of(parts, i, first, level, s)

            cells = gather_group(place, (0, 1), tile)
            pieces.append(pack_half(jnp.where(second, cells[HALF:], cells[:HALF])))
    low_west, low_east, high_west, high_east = pieces
    even_keep[...] = jnp.where(odd_strip, high_west, low_east).astype(BF)
    even_send[...] = jnp.where(odd_strip, low_west, high_east).astype(BF)
    odd_keep[...] = jnp.where(odd_strip, low_east, high_west).astype(BF)
    odd_send[...] = jnp.where(odd_strip, high_east, low_west).astype(BF)


def pack_target(at, target):
    return pl.pallas_call(
        pack_target_kernel,
        in_specs=[SCALARS, WHOLE],
        out_specs=[WHOLE] * 4,
        out_shape=[jax.ShapeDtypeStruct((PIECE, 128), BF)] * 4,
        compiler_params=PARAMS,
        name="pack_target",
    )(at, target)


WHOLE = pl.BlockSpec(memory_space=pltpu.VMEM)
SCALARS = pl.BlockSpec(memory_space=pltpu.SMEM)
HBM = pl.BlockSpec(memory_space=pltpu.HBM)
PARAMS = pltpu.CompilerParams(vmem_limit_bytes=VMEM_LIMIT)


def unpack_half_strip(half, back_ref, out_hbm, cells_s, slabs_s, semaphore):
    parts = cell_parts(1)
    slot = lax.broadcasted_iota(jnp.int32, (96, CELLS), 0)
    for block in range(2 * M):
        cells_s[block // 2, block % 2 * HALF : (block % 2 + 1) * HALF] = unpack_half(back_ref[block, :PIECE].astype(F32))
    for quad in range(2):
        groups = [cells_s[4 * quad + i].astype(BF) for i in range(4)]
        for t in range(3):
            at = 16 * (3 * quad + t)
            for level in range(2):
                slab = None
                for i in range(4):
                    if t - FIRST[i] in TILES[i]:
                        place = (place_of(parts, i, t, level, 0) == slot).astype(F32).astype(BF)
                        part = dot(place, groups[i])
                        slab = part if slab is None else slab + part
                slabs_s[level, :, at : at + 16, :] = slab.astype(BF).reshape(6, 16, C)
    copy = pltpu.make_async_copy(slabs_s, out_hbm.at[0, :, pl.ds(half * 6, 6)], semaphore)
    copy.start()
    return copy


UNPACK_SCRATCH = [
    pltpu.VMEM((M, CELLS, C), F32),
    pltpu.VMEM((2, 6, 96, C), BF),
    pltpu.SemaphoreType.DMA,
]
STRIP = jax.ShapeDtypeStruct((1, 2, 12, 96, C), BF)


def unpack_kernel(half_ref, back_ref, out_hbm, *scratch):
    unpack_half_strip(half_ref[0], back_ref, out_hbm, *scratch).wait()


def unpack(half, back):
    return pl.pallas_call(
        unpack_kernel,
        in_specs=[SCALARS, WHOLE],
        out_specs=HBM,
        out_shape=STRIP,
        scratch_shapes=UNPACK_SCRATCH,
        compiler_params=PARAMS,
        name="unpack_strip",
    )(half, back)


def split_low(total, copies):
    high = total.astype(BF)
    low = (total - high.astype(F32))[32 : 32 + LOW_ROWS].astype(BF)
    return jnp.broadcast_to(jnp.concatenate([high, low], axis=0)[None], (copies, GRAD_ROWS + LOW_ROWS, 128))


def first_sum_kernel(back_ref, out_ref):
    total = jnp.sum(back_ref[:, PIECE:].astype(F32), axis=0)
    out_ref[...] = split_low(total, out_ref.shape[0])


def second_sum_kernel(parts_ref, back_ref, out_ref):
    total = jnp.sum(parts_ref[...].astype(F32), axis=0)
    low = jnp.concatenate(
        [jnp.zeros((32, 128), F32), total[GRAD_ROWS:], jnp.zeros((GRAD_ROWS - 32 - LOW_ROWS, 128), F32)], axis=0
    )
    out_ref[:, :PIECE] = back_ref[...]
    out_ref[:, PIECE:] = split_low(total[:GRAD_ROWS] + low, out_ref.shape[0])


def finish_kernel(
    scale, per_score, half_ref, back_ref, half_done, out_hbm, qkv_out, proj_out, gain_out, loss_out, *scratch
):
    del half_done
    copy = unpack_half_strip(half_ref[0], back_ref, out_hbm, *scratch)
    pieces = [back_ref[(i + M) % (2 * M), PIECE : PIECE + GRAD_ROWS] for i in range(2 * M)]
    rows = jnp.concatenate(pieces, axis=0).astype(F32) * scale
    for i in range(4):
        qkv_out[:, 128 * i : 128 * (i + 1)] = rows[i * C : (i + 1) * C]
    rest = rows[768:864]
    qkv_out[:, 512:] = jnp.concatenate([rest[:, :64], pltpu.roll(rest, 64, 1)[:, :64]], axis=0)
    rest = rows[1056:1152]
    proj_out[:, :128] = rows[864:1056]
    proj_out[:, 128:] = jnp.concatenate([rest[:, :64], pltpu.roll(rest, 64, 1)[:, :64]], axis=0)
    piece = (1152 // GRAD_ROWS + M) % (2 * M)
    at = PIECE + 32
    extra = back_ref[piece, at : at + LOW_ROWS].astype(F32) + back_ref[piece, PIECE + GRAD_ROWS :].astype(F32)
    gain_out[...] = jnp.concatenate([extra[0:1], extra[1:2, :64]], axis=1) * scale
    loss_out[...] = (extra[2:3, 0:1] + extra[2:3, 1:2]) * per_score
    copy.wait()


def finish(half, back, half_done, count):
    return pl.pallas_call(
        functools.partial(finish_kernel, count ** (-0.5), 1.0 / (count * C)),
        in_specs=[SCALARS, WHOLE, HBM],
        out_specs=[HBM] + [WHOLE] * 4,
        out_shape=[STRIP] + [jax.ShapeDtypeStruct(shape, F32) for shape in ((C, 3 * C), (C, C), (1, C), (1, 1))],
        scratch_shapes=UNPACK_SCRATCH,
        input_output_aliases={2: 0},
        compiler_params=PARAMS,
        name="finish",
    )(half, back, half_done)


def small(kernel, name, out_shape, *args):
    return pl.pallas_call(
        kernel,
        in_specs=[WHOLE] * len(args),
        out_specs=jax.tree.map(lambda _: WHOLE, out_shape),
        out_shape=out_shape,
        compiler_params=PARAMS,
        name=name,
    )(*args)


def head_only(field, head):
    lane = lax.broadcasted_iota(jnp.int32, field.shape, 1)
    return jnp.where((lane >= head * SIZE) & (lane < (head + 1) * SIZE), field, jnp.zeros_like(field))


def main_kernel(
    at_ref, x_ref, t_ref, aux_ref, bias_ref, wkv_ref, wqkv_ref, wqkvt_ref, wproj_ref, wprojt_ref, *refs
):
    refs = list(refs)
    before_ref = refs.pop(0) if len(refs) > 18 else None
    out_ref, sums_s = refs[:2]
    (x_s, t_s, xhat_s, rstd_s, n_s, k_s, v_s, qkvt_s, attf_s, att_s, p_s, mixed_s, gat_s, tot_s, ds_s, grad_s) = refs[2:]
    sqkv_s, sproj_s, sgain_s, score_s = (
        sums_s.at[start : start + rows] for start, rows in ((0, 3 * C), (3 * C, C), (4 * C, 8), (4 * C + 8, 8))
    )
    gain_ref, valid_ref = aux_ref.at[CELLS : CELLS + 1], aux_ref.at[:CELLS]
    scale = SIZE ** (-0.5)
    to_exp2 = scale * 1.4426950408889634
    last = M - 1

    for member in range(M):
        x_s[member] = jnp.concatenate(
            [unpack_half(x_ref[member].astype(F32)), unpack_half(x_ref[M + member].astype(F32))], axis=0
        )
    kept = unpack_half(t_ref[0].astype(F32))
    received = unpack_half(t_ref[1].astype(F32))
    eastern = at_ref[0] == 1
    t_s[...] = jnp.concatenate(
        [jnp.where(eastern, received, kept), jnp.where(eastern, kept, received)], axis=0
    )

    def steps(body, unroll):
        def group(first, carry):
            for step in range(unroll):
                body(first * unroll + step)
            return carry

        whole = (M - 3) // unroll
        lax.fori_loop(0, whole, group, 0)
        for step in range(whole * unroll, M):
            body(step, min(3, last - step))


    def project_qkv(window):
        x = x_s[window]
        centred = x - jnp.mean(x, axis=1, keepdims=True)
        rstd = lax.rsqrt(jnp.mean(centred * centred, axis=1, keepdims=True) + EPS)
        xhat = centred * rstd
        xhat_s[window] = xhat
        rstd_s[window] = rstd
        normed = (xhat * gain_ref[...]).astype(BF)
        n_s[window] = normed
        kv = dot(normed, wkv_ref[...]).astype(BF)
        k_s[window] = kv[:, :C]
        v_s[window] = kv[:, C:]
        qkvt_s[window] = dot_t(wqkvt_ref[...], normed).astype(BF)

    def score_head(window, head):
        scores = dot(head_only(k_s[window], head), qkvt_s[window, :C])
        expo = jnp.exp2(scores * to_exp2 + bias_ref[...])
        p_s[window, head] = (expo * (1.0 / jnp.sum(expo, axis=0, keepdims=True))).astype(BF)

    def attend_head(window, head):
        at = slice(head * SIZE, (head + 1) * SIZE)
        attended = dot(qkvt_s[window, 2 * C + head * SIZE : 2 * C + (head + 1) * SIZE], p_s[window, head])
        attf_s[window, at] = attended
        att_s[window, at] = attended.astype(BF)

    def heads(*stages):
        for stage, window in stages:
            for head in range(HEADS):
                stage(window, head)

    def forward(step, left=3):
        projt = dot(wprojt_ref[...], att_s[step]).astype(BF)
        heads(*[(stage, step + ahead) for stage, ahead in ((attend_head, 1), (score_head, 2)) if ahead <= left])
        if left >= 3:
            project_qkv(step + 3)
        mixed_s[step] = x_s[step] + projt.T.astype(F32)

    project_qkv(0)
    heads((score_head, 0))
    project_qkv(1)
    heads((attend_head, 0), (score_head, 1))
    project_qkv(2)
    steps(forward, 5)

    def crps(step, score):
        rows = pl.ds(pl.multiple_of(step * 16, 16), 16)

        def load(ref):
            value = ref[rows]
            rest = jnp.concatenate([value[:, 128:], jnp.zeros((16, 64), F32)], axis=1)
            return jnp.concatenate([value[:, :128], rest[:8] + pltpu.roll(rest[8:], 64, 1)], axis=0)

        valid = load(valid_ref)
        target = load(t_s)
        mixed = [load(mixed_s.at[m]) for m in range(M)]
        rounded = [value.astype(BF).astype(F32) for value in mixed]
        slopes = [None] * M
        pairs = None
        for m in range(M):
            for n in range(m + 1, M):
                diff = rounded[m] - rounded[n]
                square = diff * diff + DELTA_SQ
                inverse = lax.rsqrt(square)
                size = square * inverse
                slope = diff * inverse
                pairs = size if pairs is None else pairs + size
                slopes[m] = slope if slopes[m] is None else slopes[m] + slope
                slopes[n] = -slope if slopes[n] is None else slopes[n] - slope
        total = -(2.0 * pairs + M * DELTA_SQ**0.5) / (2.0 * M)
        for m in range(M):
            diff = mixed[m] - target
            square = diff * diff + DELTA_SQ
            inverse = lax.rsqrt(square)
            total = total + square * inverse
            grad = valid * (diff * inverse - slopes[m] / M)
            rest = grad[16:]
            mixed_s[m, rows] = jnp.concatenate(
                [grad[:16], jnp.concatenate([rest[:, :64], pltpu.roll(rest, 64, 1)[:, :64]], axis=0)], axis=1
            )
        total = valid * total
        return score + (total[:8] + total[8:16] + total[16:])

    sums_s[...] = jnp.zeros_like(sums_s) if before_ref is None else before_ref[...]
    score_s[:, :128] += lax.fori_loop(0, 9, crps, jnp.zeros((8, 128), F32), unroll=9)

    def grad_attended(window):
        gat = dot_t(wproj_ref[...], mixed_s[window].astype(BF)).astype(BF)
        gat_s[window] = gat
        product = gat.astype(F32) * attf_s[window]
        for head in range(HEADS):
            tot_s[window, head] = jnp.sum(product[head * SIZE : (head + 1) * SIZE], axis=0, keepdims=True)

    def grad_score_head(window, head):
        grad_probs = dot(head_only(v_s[window], head), gat_s[window])
        ds_s[window % 4, head] = (grad_probs - tot_s[window, head]).astype(BF) * p_s[window, head]

    def grad_qkv_head(window, head):
        at = slice(head * SIZE, (head + 1) * SIZE)
        grad_scores = ds_s[window % 4, head]
        qt = qkvt_s[window, at]
        kt = qkvt_s[window, C + head * SIZE : C + (head + 1) * SIZE]
        grad_s[window, at] = (dot(kt, grad_scores) * scale).astype(BF)
        grad_s[window, C + head * SIZE : C + (head + 1) * SIZE] = (dot_t(qt, grad_scores) * scale).astype(BF)
        grad_s[window, 2 * C + head * SIZE : 2 * C + (head + 1) * SIZE] = dot_t(
            gat_s[window, at], p_s[window, head]
        ).astype(BF)

    def grad_norm(window, gbt):
        grad_normed = gbt.T.astype(F32)
        xhat = xhat_s[window]
        sgain_s[...] += jnp.sum((grad_normed * xhat).reshape(18, 8, C), axis=0)
        scaled = grad_normed * gain_ref[...]
        first = jnp.mean(scaled, axis=1, keepdims=True)
        second = jnp.mean(scaled * xhat, axis=1, keepdims=True)
        x_s[window] = mixed_s[window] + rstd_s[window] * (scaled - first - xhat * second)

    def backward(step, left=3):
        gbt = dot(wqkv_ref[...], grad_s[step]).astype(BF)
        sqkv_s[...] += dot(grad_s[step], n_s[step])
        sproj_s[...] += dot(att_s[step], mixed_s[step].astype(BF))
        heads(*[(stage, step + ahead) for stage, ahead in ((grad_qkv_head, 1), (grad_score_head, 2)) if ahead <= left])
        if left >= 3:
            grad_attended(step + 3)
        grad_norm(step, gbt)

    grad_attended(0)
    heads((grad_score_head, 0))
    grad_attended(1)
    heads((grad_qkv_head, 0), (grad_score_head, 1))
    grad_attended(2)
    steps(backward, 5)

    def pieces(member):
        return [pack_half(x_s[member, half * HALF : (half + 1) * HALF]).astype(BF) for half in range(2)]

    if before_ref is None:
        for member in range(M):
            for half, piece in enumerate(pieces(member)):
                out_ref[half * M + member] = piece
        return

    sqkv = dot_t(identity(C), sqkv_s[...].astype(BF))
    sproj = sproj_s[...]
    pad = jnp.zeros((C, 64), F32)
    rest = jnp.concatenate([sqkv[:, 512:], pad], axis=1)
    rest = rest[:96] + pltpu.roll(rest[96:], 64, 1)
    proj_rest = jnp.concatenate([sproj[:, 128:], pad], axis=1)
    proj_rest = proj_rest[:96] + pltpu.roll(proj_rest[96:], 64, 1)
    sgain = jnp.sum(sgain_s[...], axis=0, keepdims=True)
    total = jnp.sum(jnp.sum(score_s[...], axis=0, keepdims=True), axis=1, keepdims=True)
    high = total.astype(BF).astype(F32)
    low = (total - high).astype(BF).astype(F32)
    row = lax.broadcasted_iota(jnp.int32, (128, 128), 0)
    lane = lax.broadcasted_iota(jnp.int32, (128, 128), 1)
    extra = jnp.where(row == 0, jnp.broadcast_to(sgain[:, :128], (128, 128)), 0.0)
    wide = jnp.concatenate([sgain[:, 128:], jnp.zeros((1, 64), F32)], axis=1)
    extra = extra + jnp.where(row == 1, jnp.broadcast_to(wide, (128, 128)), 0.0)
    extra = extra + jnp.where((row == 2) & (lane == 0), jnp.broadcast_to(high, (128, 128)), 0.0)
    extra = extra + jnp.where((row == 2) & (lane == 1), jnp.broadcast_to(low, (128, 128)), 0.0)
    grads = jnp.concatenate(
        [sqkv[:, 128 * i : 128 * (i + 1)] for i in range(4)] + [rest, sproj[:, :128], proj_rest, extra], axis=0
    ).astype(BF)
    for member in range(M):
        for half, piece in enumerate(pieces(member)):
            to = half * M + member
            out_ref[to] = jnp.concatenate([piece, grads[to * GRAD_ROWS : (to + 1) * GRAD_ROWS]], axis=0)


SUMS = (4 * C + 16, C)


def main(at, pieces, target, aux, bias, weights, before=None):
    sums = jax.ShapeDtypeStruct(SUMS, F32)
    out = jax.ShapeDtypeStruct((2 * M, PIECE if before is None else PIECE + GRAD_ROWS, 128), BF)
    scratch = [
        pltpu.VMEM((M, CELLS, C), F32),
        pltpu.VMEM((CELLS, C), F32),
        pltpu.VMEM((M, CELLS, C), F32),
        pltpu.VMEM((M, CELLS, 1), F32),
        pltpu.VMEM((M, CELLS, C), BF),
        pltpu.VMEM((M, CELLS, C), BF),
        pltpu.VMEM((M, CELLS, C), BF),
        pltpu.VMEM((M, 3 * C, CELLS), BF),
        pltpu.VMEM((M, C, CELLS), F32),
        pltpu.VMEM((M, C, CELLS), BF),
        pltpu.VMEM((M, HEADS, CELLS, CELLS), BF),
        pltpu.VMEM((M, CELLS, C), F32),
        pltpu.VMEM((M, C, CELLS), BF),
        pltpu.VMEM((M, HEADS, 1, CELLS), F32),
        pltpu.VMEM((4, HEADS, CELLS, CELLS), BF),
        pltpu.VMEM((M, 3 * C, CELLS), BF),
    ]
    args = (at, pieces, target, aux, bias) + tuple(weights)
    if before is not None:
        scratch = [pltpu.VMEM(SUMS, F32)] + scratch
        args += (before,)
    return pl.pallas_call(
        main_kernel,
        in_specs=[SCALARS] + [WHOLE] * (len(args) - 1),
        out_specs=[WHOLE] * 2 if before is None else WHOLE,
        out_shape=[out, sums] if before is None else out,
        scratch_shapes=scratch,
        compiler_params=PARAMS,
        name="window_attention_crps",
    )(*args)


def body(inputs, target, norm_gain_vector, w_qkv, w_proj, lat_region, lat_valid):
    strips = lax.axis_size("lon")
    strip, member = lax.axis_index("lon"), lax.axis_index("mem")
    both = ("lon", "mem")

    def group(*members_of):
        return [strip * M + m for strip in members_of for m in range(M)]

    even_groups = [group(p, p + 1) for p in range(0, strips, 2)]
    odd_groups = [group(p + 1, (p + 2) % strips) for p in range(0, strips, 2)]
    alike_groups = [[(p + side) * M + m for p in range(0, strips, 2)] for side in range(2) for m in range(M)]
    even_swap = [(i, i ^ 1) for i in range(strips)]
    odd_swap = [(i, (i + 1 if i % 2 else i - 1) % strips) for i in range(strips)]

    def exchange(array, groups):
        return lax.all_to_all(array, both, 0, 0, axis_index_groups=groups)

    parity = strip % 2
    at = jnp.stack([member, parity]).astype(jnp.int32)
    side = parity.astype(jnp.int32)
    by_column = inputs.transpose(0, 1, 3, 2, 4)
    even = pack((1 - side)[None], by_column)
    even, target, by_column = lax.optimization_barrier((even, target, by_column))
    odd = pack(side[None], by_column)
    even_keep, even_send, odd_keep, odd_send = pack_target(at, target.transpose(0, 2, 1, 3))
    even = exchange(even, even_groups)
    even_target = jnp.stack([even_keep, lax.ppermute(even_send, "lon", even_swap)])
    odd_target = jnp.stack([odd_keep, lax.ppermute(odd_send, "lon", odd_swap)])

    def of_block(side):
        first = (side * M + member) * 6
        region, valid = (
            jnp.broadcast_to(lax.dynamic_slice_in_dim(rows, first, 6).reshape(1, 6, 1), (4, 6, 6)).reshape(CELLS)
            for rows in (lat_region, lat_valid)
        )
        allowed = (region[:, None] == region[None, :]) & ((valid[:, None] == 1) | np.eye(CELLS, dtype=bool))
        aux = jnp.concatenate(
            [jnp.broadcast_to(valid.astype(F32)[:, None], (CELLS, C)), jnp.broadcast_to(norm_gain_vector[None], (8, C))]
        )
        return aux, jnp.where(allowed, 0.0, -1e30).astype(F32)

    even_extra, odd_extra = (even_target, *of_block(side)), (odd_target, *of_block(1 - side))
    weights = (w_qkv[:, C:], w_qkv, w_qkv.T, w_proj, w_proj.T)
    odd, even_extra, odd_extra, weights = lax.optimization_barrier((odd, even_extra, odd_extra, weights))
    odd = exchange(odd, odd_groups)
    even_back, sums = main(side[None], even, *even_extra, weights)
    odd_back = main((1 - side)[None], odd, *odd_extra, weights, sums)
    odd_back = exchange(odd_back, odd_groups)

    count = M * 2 * 96 * 12 * strips
    rows = GRAD_ROWS + LOW_ROWS
    part = small(first_sum_kernel, "sum_group", jax.ShapeDtypeStruct((strips // 2, rows, 128), BF), odd_back)
    part = exchange(part, alike_groups)
    last = jax.ShapeDtypeStruct((2 * M, PIECE + rows, 128), BF)
    back = exchange(small(second_sum_kernel, "sum_all", last, part, even_back), even_groups)
    half_done = unpack(side[None], odd_back)
    by_column, grad_qkv, grad_proj, grad_gain, loss = finish((1 - side)[None], back, half_done, count)
    grad_inputs = by_column.transpose(0, 1, 3, 2, 4)
    return (grad_inputs, grad_qkv, grad_proj, grad_gain[0], loss[0, 0])


def solution(mesh):
    in_specs = (
        P("mem", None, None, "lon", None),
        P(None, None, "lon", None),
        P(),
        P(),
        P(),
        P(),
        P(),
    )
    out_specs = (P("mem", None, None, "lon", None), P(), P(), P(), P())
    return jax.shard_map(body, mesh=mesh, in_specs=in_specs, out_specs=out_specs, check_vma=False)
```

```python
import functools

import jax
import jax.numpy as jnp
import numpy as np
from jax import lax
from jax.experimental import pallas as pl
from jax.experimental.pallas import tpu as pltpu
from jax.sharding import PartitionSpec as P

HEADS = 6
SIZE = 32
SHIFT = 6
C = 192
CELLS = 144
HALF = 72
M = 8
EPS = 1e-05
DELTA_SQ = 0.0625
PIECE = 112
GRAD_ROWS = 80
LOW_ROWS = 16
BF = jnp.bfloat16
F32 = jnp.float32
VMEM_LIMIT = 40 * 1024 * 1024


def dot(left, right):
    return jnp.dot(left, right, preferred_element_type=F32)


def dot_t(left, right):
    return lax.dot_general(left, right, (((1,), (1,)), ((), ())), preferred_element_type=F32)


def identity(n):
    return (
        lax.broadcasted_iota(jnp.int32, (n, n), 0) == lax.broadcasted_iota(jnp.int32, (n, n), 1)
    ).astype(BF)


def pack_half(cells):
    rest = jnp.concatenate([cells[:, 128:], jnp.zeros((HALF, 64), F32)], axis=1)
    second = jnp.concatenate([rest[40:], jnp.zeros((8, 128), F32)], axis=0)
    return jnp.concatenate([cells[:, :128], rest[:40] + pltpu.roll(second, 64, 1)], axis=0)


def unpack_half(piece):
    rest = piece[HALF:]
    rest = jnp.concatenate([rest[:, :64], pltpu.roll(rest, 64, 1)[:32, :64]], axis=0)
    return jnp.concatenate([piece[:HALF], rest], axis=1)


TILES = ((0,), (0, 1), (0, 1), (1,))
FIRST = (0, 0, 1, 1)


def cell_parts(axis):
    cell = lax.broadcasted_iota(jnp.int32, (CELLS, 1) if axis == 0 else (1, CELLS), axis)
    block = (cell >= 72).astype(jnp.int32)
    cell = cell - 72 * block
    level = (cell >= 36).astype(jnp.int32)
    cell = cell - 36 * level
    row = sum((cell >= 6 * k).astype(jnp.int32) for k in range(1, 6))
    return 6 * block + row, level, cell - 6 * row


def place_of(parts, i, first, level, s):
    row, its_level, column = parts
    lat = 12 * i + row - 16 * (first + s)
    return jnp.where((lat >= 0) & (lat < 16) & (its_level == level), column * 16 + lat, -1)


def gather_group(place, steps, tile):
    lane = lax.broadcasted_iota(jnp.int32, (CELLS, 96), 1)
    cells = None
    for s in steps:
        for level in range(2):
            part = dot((place(level, s) == lane).astype(F32).astype(BF), tile(level, s))
            cells = part if cells is None else cells + part
    return cells


def pack_kernel(x_ref, out_ref):
    parts = cell_parts(0)
    for quad in range(2):
        for i in range(4):

            def tile(level, s):
                at = 16 * (3 * quad + FIRST[i] + s)
                return x_ref[0, level, :, at : at + 16, :].reshape(96, C)

            def place(level, s):
                return place_of(parts, i, FIRST[i], level, s)

            cells = gather_group(place, TILES[i], tile)
            for sub in range(2):
                out_ref[8 * quad + 2 * i + sub] = pack_half(cells[sub * HALF : (sub + 1) * HALF]).astype(BF)


def pack(half, inputs):
    return pl.pallas_call(
        pack_kernel,
        in_specs=[WHOLE],
        out_specs=WHOLE,
        out_shape=jax.ShapeDtypeStruct((2 * M, PIECE, 128), BF),
        compiler_params=PARAMS,
        name="pack_strip",
    )(lax.dynamic_slice_in_dim(inputs, half * 6, 6, axis=2))


def pack_target_kernel(at_ref, t_ref, even_keep, even_send, odd_keep, odd_send):
    member, odd_strip = at_ref[0], at_ref[1] == 1
    i = member // 2
    first = jnp.where(i >= 2, 1, 0)
    second = member % 2 == 1
    parts = cell_parts(0)
    pieces = []
    for quad in range(2):
        for half in range(2):

            def tile(level, s):
                at = pl.multiple_of(16 * (3 * quad + first + s), 16)
                return t_ref[level, 6 * half : 6 * half + 6, pl.ds(at, 16), :].reshape(96, C)

            def place(level, s):
                return place_of(parts, i, first, level, s)

            cells = gather_group(place, (0, 1), tile)
            pieces.append(pack_half(jnp.where(second, cells[HALF:], cells[:HALF])))
    low_west, low_east, high_west, high_east = pieces
    even_keep[...] = jnp.where(odd_strip, high_west, low_east).astype(BF)
    even_send[...] = jnp.where(odd_strip, low_west, high_east).astype(BF)
    odd_keep[...] = jnp.where(odd_strip, low_east, high_west).astype(BF)
    odd_send[...] = jnp.where(odd_strip, high_east, low_west).astype(BF)


def pack_target(at, target):
    return pl.pallas_call(
        pack_target_kernel,
        in_specs=[SCALARS, WHOLE],
        out_specs=[WHOLE] * 4,
        out_shape=[jax.ShapeDtypeStruct((PIECE, 128), BF)] * 4,
        compiler_params=PARAMS,
        name="pack_target",
    )(at, target)


WHOLE = pl.BlockSpec(memory_space=pltpu.VMEM)
SCALARS = pl.BlockSpec(memory_space=pltpu.SMEM)
HBM = pl.BlockSpec(memory_space=pltpu.HBM)
PARAMS = pltpu.CompilerParams(vmem_limit_bytes=VMEM_LIMIT)


def unpack_half_strip(half, back_ref, out_hbm, cells_s, slabs_s, semaphore):
    parts = cell_parts(1)
    slot = lax.broadcasted_iota(jnp.int32, (96, CELLS), 0)
    for block in range(2 * M):
        cells_s[block // 2, block % 2 * HALF : (block % 2 + 1) * HALF] = unpack_half(back_ref[block, :PIECE].astype(F32))
    for quad in range(2):
        groups = [cells_s[4 * quad + i].astype(BF) for i in range(4)]
        for t in range(3):
            at = 16 * (3 * quad + t)
            for level in range(2):
                slab = None
                for i in range(4):
                    if t - FIRST[i] in TILES[i]:
                        place = (place_of(parts, i, t, level, 0) == slot).astype(F32).astype(BF)
                        part = dot(place, groups[i])
                        slab = part if slab is None else slab + part
                slabs_s[level, :, at : at + 16, :] = slab.astype(BF).reshape(6, 16, C)
    copy = pltpu.make_async_copy(slabs_s, out_hbm.at[0, :, pl.ds(half * 6, 6)], semaphore)
    copy.start()
    return copy


UNPACK_SCRATCH = [
    pltpu.VMEM((M, CELLS, C), F32),
    pltpu.VMEM((2, 6, 96, C), BF),
    pltpu.SemaphoreType.DMA,
]
STRIP = jax.ShapeDtypeStruct((1, 2, 12, 96, C), BF)


def unpack_kernel(half_ref, back_ref, out_hbm, *scratch):
    unpack_half_strip(half_ref[0], back_ref, out_hbm, *scratch).wait()


def unpack(half, back):
    return pl.pallas_call(
        unpack_kernel,
        in_specs=[SCALARS, WHOLE],
        out_specs=HBM,
        out_shape=STRIP,
        scratch_shapes=UNPACK_SCRATCH,
        compiler_params=PARAMS,
        name="unpack_strip",
    )(half, back)


def split_low(total, copies):
    high = total.astype(BF)
    low = (total - high.astype(F32))[32 : 32 + LOW_ROWS].astype(BF)
    return jnp.broadcast_to(jnp.concatenate([high, low], axis=0)[None], (copies, GRAD_ROWS + LOW_ROWS, 128))


def first_sum_kernel(back_ref, out_ref):
    total = jnp.sum(back_ref[:, PIECE:].astype(F32), axis=0)
    out_ref[...] = split_low(total, out_ref.shape[0])


def second_sum_kernel(parts_ref, back_ref, out_ref):
    total = jnp.sum(parts_ref[...].astype(F32), axis=0)
    low = jnp.concatenate(
        [jnp.zeros((32, 128), F32), total[GRAD_ROWS:], jnp.zeros((GRAD_ROWS - 32 - LOW_ROWS, 128), F32)], axis=0
    )
    out_ref[:, :PIECE] = back_ref[...]
    out_ref[:, PIECE:] = split_low(total[:GRAD_ROWS] + low, out_ref.shape[0])


def finish_kernel(
    scale, per_score, half_ref, back_ref, half_done, out_hbm, qkv_out, proj_out, gain_out, loss_out, *scratch
):
    del half_done
    copy = unpack_half_strip(half_ref[0], back_ref, out_hbm, *scratch)
    pieces = [back_ref[(i + M) % (2 * M), PIECE : PIECE + GRAD_ROWS] for i in range(2 * M)]
    rows = jnp.concatenate(pieces, axis=0).astype(F32) * scale
    for i in range(4):
        qkv_out[:, 128 * i : 128 * (i + 1)] = rows[i * C : (i + 1) * C]
    rest = rows[768:864]
    qkv_out[:, 512:] = jnp.concatenate([rest[:, :64], pltpu.roll(rest, 64, 1)[:, :64]], axis=0)
    rest = rows[1056:1152]
    proj_out[:, :128] = rows[864:1056]
    proj_out[:, 128:] = jnp.concatenate([rest[:, :64], pltpu.roll(rest, 64, 1)[:, :64]], axis=0)
    piece = (1152 // GRAD_ROWS + M) % (2 * M)
    at = PIECE + 32
    extra = back_ref[piece, at : at + LOW_ROWS].astype(F32) + back_ref[piece, PIECE + GRAD_ROWS :].astype(F32)
    gain_out[...] = jnp.concatenate([extra[0:1], extra[1:2, :64]], axis=1) * scale
    loss_out[...] = (extra[2:3, 0:1] + extra[2:3, 1:2]) * per_score
    copy.wait()


def finish(half, back, half_done, count):
    return pl.pallas_call(
        functools.partial(finish_kernel, count ** (-0.5), 1.0 / (count * C)),
        in_specs=[SCALARS, WHOLE, HBM],
        out_specs=[HBM] + [WHOLE] * 4,
        out_shape=[STRIP] + [jax.ShapeDtypeStruct(shape, F32) for shape in ((C, 3 * C), (C, C), (1, C), (1, 1))],
        scratch_shapes=UNPACK_SCRATCH,
        input_output_aliases={2: 0},
        compiler_params=PARAMS,
        name="finish",
    )(half, back, half_done)


def small(kernel, name, out_shape, *args):
    return pl.pallas_call(
        kernel,
        in_specs=[WHOLE] * len(args),
        out_specs=jax.tree.map(lambda _: WHOLE, out_shape),
        out_shape=out_shape,
        compiler_params=PARAMS,
        name=name,
    )(*args)


def head_only(field, head):
    lane = lax.broadcasted_iota(jnp.int32, field.shape, 1)
    return jnp.where((lane >= head * SIZE) & (lane < (head + 1) * SIZE), field, jnp.zeros_like(field))


def main_kernel(
    at_ref, x_ref, t_ref, aux_ref, bias_ref, wkv_ref, wqkv_ref, wqkvt_ref, wproj_ref, wprojt_ref, *refs
):
    refs = list(refs)
    before_ref = refs.pop(0) if len(refs) > 18 else None
    out_ref, sums_s = refs[:2]
    (x_s, t_s, xhat_s, rstd_s, n_s, k_s, v_s, qkvt_s, attf_s, att_s, p_s, mixed_s, gat_s, tot_s, ds_s, grad_s) = refs[2:]
    sqkv_s, sproj_s, sgain_s, score_s = (
        sums_s.at[start : start + rows] for start, rows in ((0, 3 * C), (3 * C, C), (4 * C, 8), (4 * C + 8, 8))
    )
    gain_ref, valid_ref = aux_ref.at[CELLS : CELLS + 1], aux_ref.at[:CELLS]
    scale = SIZE ** (-0.5)
    to_exp2 = scale * 1.4426950408889634
    last = M - 1

    for member in range(M):
        x_s[member] = jnp.concatenate(
            [unpack_half(x_ref[member].astype(F32)), unpack_half(x_ref[M + member].astype(F32))], axis=0
        )
    kept = unpack_half(t_ref[0].astype(F32))
    received = unpack_half(t_ref[1].astype(F32))
    eastern = at_ref[0] == 1
    t_s[...] = jnp.concatenate(
        [jnp.where(eastern, received, kept), jnp.where(eastern, kept, received)], axis=0
    )

    def steps(body, unroll):
        def group(first, carry):
            for step in range(unroll):
                body(first * unroll + step)
            return carry

        whole = (M - 3) // unroll
        lax.fori_loop(0, whole, group, 0)
        for step in range(whole * unroll, M):
            body(step, min(3, last - step))


    def project_qkv(window):
        x = x_s[window]
        centred = x - jnp.mean(x, axis=1, keepdims=True)
        rstd = lax.rsqrt(jnp.mean(centred * centred, axis=1, keepdims=True) + EPS)
        xhat = centred * rstd
        xhat_s[window] = xhat
        rstd_s[window] = rstd
        normed = (xhat * gain_ref[...]).astype(BF)
        n_s[window] = normed
        kv = dot(normed, wkv_ref[...]).astype(BF)
        k_s[window] = kv[:, :C]
        v_s[window] = kv[:, C:]
        qkvt_s[window] = dot_t(wqkvt_ref[...], normed).astype(BF)

    def score_head(window, head):
        scores = dot(head_only(k_s[window], head), qkvt_s[window, :C])
        expo = jnp.exp2(scores * to_exp2 + bias_ref[...])
        p_s[window, head] = (expo * (1.0 / jnp.sum(expo, axis=0, keepdims=True))).astype(BF)

    def attend_head(window, head):
        at = slice(head * SIZE, (head + 1) * SIZE)
        attended = dot(qkvt_s[window, 2 * C + head * SIZE : 2 * C + (head + 1) * SIZE], p_s[window, head])
        attf_s[window, at] = attended
        att_s[window, at] = attended.astype(BF)

    def heads(*stages):
        for stage, window in stages:
            for head in range(HEADS):
                stage(window, head)

    def forward(step, left=3):
        projt = dot(wprojt_ref[...], att_s[step]).astype(BF)
        heads(*[(stage, step + ahead) for stage, ahead in ((attend_head, 1), (score_head, 2)) if ahead <= left])
        if left >= 3:
            project_qkv(step + 3)
        mixed_s[step] = x_s[step] + projt.T.astype(F32)

    project_qkv(0)
    heads((score_head, 0))
    project_qkv(1)
    heads((attend_head, 0), (score_head, 1))
    project_qkv(2)
    steps(forward, 5)

    def crps(step, score):
        rows = pl.ds(pl.multiple_of(step * 16, 16), 16)

        def load(ref):
            value = ref[rows]
            rest = jnp.concatenate([value[:, 128:], jnp.zeros((16, 64), F32)], axis=1)
            return jnp.concatenate([value[:, :128], rest[:8] + pltpu.roll(rest[8:], 64, 1)], axis=0)

        valid = load(valid_ref)
        target = load(t_s)
        mixed = [load(mixed_s.at[m]) for m in range(M)]
        rounded = [value.astype(BF).astype(F32) for value in mixed]
        slopes = [None] * M
        pairs = None
        for m in range(M):
            for n in range(m + 1, M):
                diff = rounded[m] - rounded[n]
                square = diff * diff + DELTA_SQ
                inverse = lax.rsqrt(square)
                size = square * inverse
                slope = diff * inverse
                pairs = size if pairs is None else pairs + size
                slopes[m] = slope if slopes[m] is None else slopes[m] + slope
                slopes[n] = -slope if slopes[n] is None else slopes[n] - slope
        total = -(2.0 * pairs + M * DELTA_SQ**0.5) / (2.0 * M)
        for m in range(M):
            diff = mixed[m] - target
            square = diff * diff + DELTA_SQ
            inverse = lax.rsqrt(square)
            total = total + square * inverse
            grad = valid * (diff * inverse - slopes[m] / M)
            rest = grad[16:]
            mixed_s[m, rows] = jnp.concatenate(
                [grad[:16], jnp.concatenate([rest[:, :64], pltpu.roll(rest, 64, 1)[:, :64]], axis=0)], axis=1
            )
        total = valid * total
        return score + (total[:8] + total[8:16] + total[16:])

    sums_s[...] = jnp.zeros_like(sums_s) if before_ref is None else before_ref[...]
    score_s[:, :128] += lax.fori_loop(0, 9, crps, jnp.zeros((8, 128), F32), unroll=9)

    def grad_attended(window):
        gat = dot_t(wproj_ref[...], mixed_s[window].astype(BF)).astype(BF)
        gat_s[window] = gat
        product = gat.astype(F32) * attf_s[window]
        for head in range(HEADS):
            tot_s[window, head] = jnp.sum(product[head * SIZE : (head + 1) * SIZE], axis=0, keepdims=True)

    def grad_score_head(window, head):
        grad_probs = dot(head_only(v_s[window], head), gat_s[window])
        ds_s[window % 4, head] = (grad_probs - tot_s[window, head]).astype(BF) * p_s[window, head]

    def grad_qkv_head(window, head):
        at = slice(head * SIZE, (head + 1) * SIZE)
        grad_scores = ds_s[window % 4, head]
        qt = qkvt_s[window, at]
        kt = qkvt_s[window, C + head * SIZE : C + (head + 1) * SIZE]
        grad_s[window, at] = (dot(kt, grad_scores) * scale).astype(BF)
        grad_s[window, C + head * SIZE : C + (head + 1) * SIZE] = (dot_t(qt, grad_scores) * scale).astype(BF)
        grad_s[window, 2 * C + head * SIZE : 2 * C + (head + 1) * SIZE] = dot_t(
            gat_s[window, at], p_s[window, head]
        ).astype(BF)

    def grad_norm(window, gbt):
        grad_normed = gbt.T.astype(F32)
        xhat = xhat_s[window]
        sgain_s[...] += jnp.sum((grad_normed * xhat).reshape(18, 8, C), axis=0)
        scaled = grad_normed * gain_ref[...]
        first = jnp.mean(scaled, axis=1, keepdims=True)
        second = jnp.mean(scaled * xhat, axis=1, keepdims=True)
        x_s[window] = mixed_s[window] + rstd_s[window] * (scaled - first - xhat * second)

    def backward(step, left=3):
        gbt = dot(wqkv_ref[...], grad_s[step]).astype(BF)
        sqkv_s[...] += dot(grad_s[step], n_s[step])
        sproj_s[...] += dot(att_s[step], mixed_s[step].astype(BF))
        heads(*[(stage, step + ahead) for stage, ahead in ((grad_qkv_head, 1), (grad_score_head, 2)) if ahead <= left])
        if left >= 3:
            grad_attended(step + 3)
        grad_norm(step, gbt)

    grad_attended(0)
    heads((grad_score_head, 0))
    grad_attended(1)
    heads((grad_qkv_head, 0), (grad_score_head, 1))
    grad_attended(2)
    steps(backward, 5)

    def pieces(member):
        return [pack_half(x_s[member, half * HALF : (half + 1) * HALF]).astype(BF) for half in range(2)]

    if before_ref is None:
        for member in range(M):
            for half, piece in enumerate(pieces(member)):
                out_ref[half * M + member] = piece
        return

    sqkv = dot_t(identity(C), sqkv_s[...].astype(BF))
    sproj = sproj_s[...]
    pad = jnp.zeros((C, 64), F32)
    rest = jnp.concatenate([sqkv[:, 512:], pad], axis=1)
    rest = rest[:96] + pltpu.roll(rest[96:], 64, 1)
    proj_rest = jnp.concatenate([sproj[:, 128:], pad], axis=1)
    proj_rest = proj_rest[:96] + pltpu.roll(proj_rest[96:], 64, 1)
    sgain = jnp.sum(sgain_s[...], axis=0, keepdims=True)
    total = jnp.sum(jnp.sum(score_s[...], axis=0, keepdims=True), axis=1, keepdims=True)
    high = total.astype(BF).astype(F32)
    low = (total - high).astype(BF).astype(F32)
    row = lax.broadcasted_iota(jnp.int32, (128, 128), 0)
    lane = lax.broadcasted_iota(jnp.int32, (128, 128), 1)
    extra = jnp.where(row == 0, jnp.broadcast_to(sgain[:, :128], (128, 128)), 0.0)
    wide = jnp.concatenate([sgain[:, 128:], jnp.zeros((1, 64), F32)], axis=1)
    extra = extra + jnp.where(row == 1, jnp.broadcast_to(wide, (128, 128)), 0.0)
    extra = extra + jnp.where((row == 2) & (lane == 0), jnp.broadcast_to(high, (128, 128)), 0.0)
    extra = extra + jnp.where((row == 2) & (lane == 1), jnp.broadcast_to(low, (128, 128)), 0.0)
    grads = jnp.concatenate(
        [sqkv[:, 128 * i : 128 * (i + 1)] for i in range(4)] + [rest, sproj[:, :128], proj_rest, extra], axis=0
    ).astype(BF)
    for member in range(M):
        for half, piece in enumerate(pieces(member)):
            to = half * M + member
            out_ref[to] = jnp.concatenate([piece, grads[to * GRAD_ROWS : (to + 1) * GRAD_ROWS]], axis=0)


SUMS = (4 * C + 16, C)


def main(at, pieces, target, aux, bias, weights, before=None):
    sums = jax.ShapeDtypeStruct(SUMS, F32)
    out = jax.ShapeDtypeStruct((2 * M, PIECE if before is None else PIECE + GRAD_ROWS, 128), BF)
    scratch = [
        pltpu.VMEM((M, CELLS, C), F32),
        pltpu.VMEM((CELLS, C), F32),
        pltpu.VMEM((M, CELLS, C), F32),
        pltpu.VMEM((M, CELLS, 1), F32),
        pltpu.VMEM((M, CELLS, C), BF),
        pltpu.VMEM((M, CELLS, C), BF),
        pltpu.VMEM((M, CELLS, C), BF),
        pltpu.VMEM((M, 3 * C, CELLS), BF),
        pltpu.VMEM((M, C, CELLS), F32),
        pltpu.VMEM((M, C, CELLS), BF),
        pltpu.VMEM((M, HEADS, CELLS, CELLS), BF),
        pltpu.VMEM((M, CELLS, C), F32),
        pltpu.VMEM((M, C, CELLS), BF),
        pltpu.VMEM((M, HEADS, 1, CELLS), F32),
        pltpu.VMEM((4, HEADS, CELLS, CELLS), BF),
        pltpu.VMEM((M, 3 * C, CELLS), BF),
    ]
    args = (at, pieces, target, aux, bias) + tuple(weights)
    if before is not None:
        scratch = [pltpu.VMEM(SUMS, F32)] + scratch
        args += (before,)
    return pl.pallas_call(
        main_kernel,
        in_specs=[SCALARS] + [WHOLE] * (len(args) - 1),
        out_specs=[WHOLE] * 2 if before is None else WHOLE,
        out_shape=[out, sums] if before is None else out,
        scratch_shapes=scratch,
        compiler_params=PARAMS,
        name="window_attention_crps",
    )(*args)


def body(inputs, target, norm_gain_vector, w_qkv, w_proj, lat_region, lat_valid):
    strips = lax.axis_size("lon")
    strip, member = lax.axis_index("lon"), lax.axis_index("mem")
    both = ("lon", "mem")

    def group(*members_of):
        return [strip * M + m for strip in members_of for m in range(M)]

    even_groups = [group(p, p + 1) for p in range(0, strips, 2)]
    odd_groups = [group(p + 1, (p + 2) % strips) for p in range(0, strips, 2)]
    alike_groups = [[(p + side) * M + m for p in range(0, strips, 2)] for side in range(2) for m in range(M)]
    even_swap = [(i, i ^ 1) for i in range(strips)]
    odd_swap = [(i, (i + 1 if i % 2 else i - 1) % strips) for i in range(strips)]

    def exchange(array, groups):
        return lax.all_to_all(array, both, 0, 0, axis_index_groups=groups)

    parity = strip % 2
    at = jnp.stack([member, parity]).astype(jnp.int32)
    side = parity.astype(jnp.int32)
    by_column = inputs.transpose(0, 1, 3, 2, 4)
    even = pack(1 - side, by_column)
    even, target, by_column = lax.optimization_barrier((even, target, by_column))
    odd = pack(side, by_column)
    even_keep, even_send, odd_keep, odd_send = pack_target(at, target.transpose(0, 2, 1, 3))
    even = exchange(even, even_groups)
    even_target = jnp.stack([even_keep, lax.ppermute(even_send, "lon", even_swap)])
    odd_target = jnp.stack([odd_keep, lax.ppermute(odd_send, "lon", odd_swap)])

    def of_block(side):
        first = (side * M + member) * 6
        region, valid = (
            jnp.broadcast_to(lax.dynamic_slice_in_dim(rows, first, 6).reshape(1, 6, 1), (4, 6, 6)).reshape(CELLS)
            for rows in (lat_region, lat_valid)
        )
        allowed = (region[:, None] == region[None, :]) & ((valid[:, None] == 1) | np.eye(CELLS, dtype=bool))
        aux = jnp.concatenate(
            [jnp.broadcast_to(valid.astype(F32)[:, None], (CELLS, C)), jnp.broadcast_to(norm_gain_vector[None], (8, C))]
        )
        return aux, jnp.where(allowed, 0.0, -1e30).astype(F32)

    even_extra, odd_extra = (even_target, *of_block(side)), (odd_target, *of_block(1 - side))
    weights = (w_qkv[:, C:], w_qkv, w_qkv.T, w_proj, w_proj.T)
    odd, even_extra, odd_extra, weights = lax.optimization_barrier((odd, even_extra, odd_extra, weights))
    odd = exchange(odd, odd_groups)
    even_back, sums = main(side[None], even, *even_extra, weights)
    odd_back = main((1 - side)[None], odd, *odd_extra, weights, sums)
    odd_back = exchange(odd_back, odd_groups)

    count = M * 2 * 96 * 12 * strips
    rows = GRAD_ROWS + LOW_ROWS
    part = small(first_sum_kernel, "sum_group", jax.ShapeDtypeStruct((strips // 2, rows, 128), BF), odd_back)
    part = exchange(part, alike_groups)
    last = jax.ShapeDtypeStruct((2 * M, PIECE + rows, 128), BF)
    back = exchange(small(second_sum_kernel, "sum_all", last, part, even_back), even_groups)
    half_done = unpack(side[None], odd_back)
    by_column, grad_qkv, grad_proj, grad_gain, loss = finish((1 - side)[None], back, half_done, count)
    grad_inputs = by_column.transpose(0, 1, 3, 2, 4)
    return (grad_inputs, grad_qkv, grad_proj, grad_gain[0], loss[0, 0])


def solution(mesh):
    in_specs = (
        P("mem", None, None, "lon", None),
        P(None, None, "lon", None),
        P(),
        P(),
        P(),
        P(),
        P(),
    )
    out_specs = (P("mem", None, None, "lon", None), P(), P(), P(), P())
    return jax.shard_map(body, mesh=mesh, in_specs=in_specs, out_specs=out_specs, check_vma=False)
```
